128 devices in a mesh: row: 16 (over z, y), col: 8 (over x, core).
Axes of the slice: x: 4, y: 4, z: 4, core: 2. Of those that a mesh axis runs over, the one named last changes fastest.
Arguments:
- rhs: float32 [131072, 256], P(('row', 'col')), may hold values from -8 to 8
- front_factor: float32 [131072, 1024], P(('row', 'col')), may hold values from -1 to 4, as said below
- coupling: bfloat16 [229376, 1024], P(('row', 'col')), may hold values from -0.1875 to 0.1875
- bound_count: int32 [128], P(('row', 'col')), may hold values from 448 to 1792, as said below
- sep_owner: int32 [128, 64], P(('row', 'col')), may hold values from 0 to 127, as said below
- sep_index: int32 [128, 1792], P(('row', 'col')), may hold values from 0 to 511
- sep_rhs: float32 [65536, 256], P(('row', 'col')), may hold values from -6 to 6
- sep_factor: float32 [65536, 512], P(('row', 'col')), may hold values from -1 to 4, as said below
- cell_weight: float32 [16384, 8], P(('row', 'col')), may hold values from 0.02 to 0.3
- cell_pivot: int32 [16384, 8], P(('row', 'col')), may hold values from 0 to 1023
Outputs:
- sep_potential: float32 [65536, 256], P(('row', 'col'))
- hess: float32 [16384, 16384], P('row', 'col')
The draws below stay inside these ranges and needn't reach their ends.
Inputs may be any that keep to these rules, and one draw needn't show every extreme that they name: `front_factor`: each block of 1024 rows is lower triangular with diagonal entries 1 or more. `sep_factor`: each block of 512 rows is lower triangular with diagonal entries 1 or more. `bound_count`: some front has all 1792 boundary rows live. `sep_owner`: each row names 64 distinct separator blocks.
All inputs are finite; a program needn't handle non-finite values.
Results may differ from the reference program's by a relative error of at most 0.0031.
Values may be sent and summed in bfloat16 or wider, within the bound.
No kernel may reach another device: no remote copies, remote signals or barrier semaphores. Data moves between devices by JAX's collectives and lax.ppermute only.
A program may use at most 128 MiB of HBM per device.

```python
import math
import jax
import jax.numpy as jnp
from jax import lax

P_SIZE = 1024
B = 1792
S = 256
SEP = 512
CELL_DEV = 128
NNZ = 8
FRONTS = 128
CELLS = 16384
N_ROW = 16
N_COL = 8


def lower_blocks(key, count, order):
    first, second = jax.random.split(key)
    diagonal = jax.random.uniform(first, (count, order), jnp.float32, 1.0, 2.0)
    spread = jnp.clip(jax.random.normal(second, (count, order, order), jnp.float32), -6.0, 6.0)
    lower = jnp.tril(spread * (0.5 / math.sqrt(order)), -1)
    whole = lower + diagonal[:, :, None] * jnp.eye(order, dtype=jnp.float32)[None, :, :]
    return whole.reshape(count * order, order)


def draw_rhs(key, part):
    first, second = jax.random.split(jax.random.fold_in(key, 11))
    common = jnp.clip(jax.random.normal(first, (1, S), jnp.float32), -3.0, 3.0)
    noise = jax.random.normal(second, (FRONTS * P_SIZE, S), jnp.float32)
    return jnp.clip(common + noise, -8.0, 8.0)


def draw_front_factor(key, part):
    return lower_blocks(jax.random.fold_in(key, 23), FRONTS, P_SIZE)


def draw_sep_factor(key, part):
    return lower_blocks(jax.random.fold_in(key, 37), FRONTS, SEP)


def draw_bound_count(key, part):
    first, second = jax.random.split(jax.random.fold_in(key, 41))
    counts = jax.random.randint(first, (FRONTS,), B // 4, B + 1, dtype=jnp.int32)
    chosen = jax.random.randint(second, (), 0, FRONTS, dtype=jnp.int32)
    return counts.at[chosen].set(B)


def draw_sep_owner(key, part):
    keys = jax.random.split(jax.random.fold_in(key, 53), FRONTS)
    orders = jax.vmap(lambda single: jax.random.permutation(single, FRONTS))(keys)
    return orders[:, :FRONTS // 2].astype(jnp.int32)


def set_ends(entries, own_key, smallest, high):
    shape = entries.shape
    spot = [jax.random.randint(jax.random.fold_in(own_key, axis), (), 0, shape[axis]) for axis in range(len(shape))]
    entries = entries.at[tuple(spot)].set(smallest)
    longest = shape.index(max(shape))
    spot[longest] = (spot[longest] + 1) % shape[longest]
    return entries.at[tuple(spot)].set(high)


def shard_levels(key, extent, cuts, smallest, largest):
    factor_of, own = 1.0, jax.random.fold_in(key, 6)
    for axis_at, shards_of in cuts:
        heights = jnp.exp(jax.random.uniform(jax.random.fold_in(own, axis_at), (shards_of,), jnp.float32, smallest / len(cuts), largest / len(cuts)))
        factor_of = factor_of * jnp.repeat(heights, extent[axis_at] // shards_of).reshape([-1 if axis == axis_at else 1 for axis in range(len(extent))])
    return factor_of


def gaussian(own_key, shape, deviation, bound, shards=(), kind=jnp.bfloat16):
    drawn = jax.random.normal(own_key, shape, jnp.float32) * deviation
    if len(shards) > 0:
        drawn = shard_levels(own_key, shape, shards, -0.22, 0.18) * drawn
    return jnp.clip(drawn, min=-bound, max=bound).astype(kind)


def setup_inputs(seed: int = 0) -> dict:
    seeds = jax.random.split(jax.random.key(seed), 11)
    return {
        "rhs": draw_rhs(jax.random.fold_in(seeds[10], 71), 0),
        "front_factor": draw_front_factor(jax.random.fold_in(seeds[10], 71), 0),
        "coupling": gaussian(seeds[2], (FRONTS * B, P_SIZE), P_SIZE ** -0.5, 0.1875, ((0, 128),)),
        "bound_count": draw_bound_count(jax.random.fold_in(seeds[10], 71), 0),
        "sep_owner": draw_sep_owner(jax.random.fold_in(seeds[10], 71), 0),
        "sep_index": set_ends(jax.random.randint(seeds[5], (FRONTS, B), 0, SEP), jax.random.fold_in(seeds[5], 1), 0, SEP - 1).astype(jnp.int32),
        "sep_rhs": gaussian(seeds[6], (FRONTS * SEP, S), 1.0, 6.0, ((0, 128),), jnp.float32),
        "sep_factor": draw_sep_factor(jax.random.fold_in(seeds[10], 71), 0),
        "cell_weight": jnp.clip(jnp.exp(math.log(0.3) - 2.7080503 * jax.random.uniform(seeds[8], (CELLS, NNZ), jnp.float32) ** shard_levels(seeds[8], (CELLS, NNZ), ((0, 128),), -0.2, 0.2)), 0.02, 0.3),
        "cell_pivot": set_ends(jax.random.randint(seeds[9], (CELLS, NNZ), 0, P_SIZE), jax.random.fold_in(seeds[9], 1), 0, P_SIZE - 1).astype(jnp.int32),
    }


def front_solve(factor, right):
    half_way = jax.scipy.linalg.solve_triangular(factor, right, lower=True)
    return jax.scipy.linalg.solve_triangular(factor, half_way, trans=1, lower=True)

def reference(rhs, front_factor, coupling, bound_count, sep_owner, sep_index, sep_rhs, sep_factor, cell_weight, cell_pivot):
    fronts = N_ROW * N_COL
    halves = fronts // 2
    slots = B // halves
    factors = front_factor.reshape(fronts, P_SIZE, P_SIZE)
    rights = rhs.reshape(fronts, P_SIZE, S)
    blocks = coupling.reshape(fronts, B, P_SIZE)
    living = jnp.arange(B, dtype=jnp.int32)[None, :] < bound_count[:, None]
    live_float = living.astype(jnp.float32)
    live_half = living.astype(jnp.bfloat16)
    slot_owner = jnp.repeat(sep_owner, slots, axis=1)
    global_index = (slot_owner * SEP + sep_index).astype(jnp.int32)

    def forward(inputs):
        factor, right, block, marks = inputs
        solved = front_solve(factor, right).astype(jnp.bfloat16)
        product = jnp.dot(block.astype(jnp.float32), solved.astype(jnp.float32), preferred_element_type=jnp.float32)
        return (product * marks[:, None]).astype(jnp.bfloat16)
    contrib = lax.map(forward, (factors, rights, blocks, live_float))
    totals = jnp.zeros((fronts * SEP, S), jnp.float32).at[global_index.reshape(-1)].add(contrib.reshape(-1, S).astype(jnp.float32))
    reduced = (sep_rhs - totals).reshape(fronts, SEP, S)
    sep_blocks = sep_factor.reshape(fronts, SEP, SEP)

    def separator(inputs):
        return front_solve(inputs[0], inputs[1])
    sep_potential = lax.map(separator, (sep_blocks, reduced)).reshape(fronts * SEP, S)
    sep_half = sep_potential.astype(jnp.bfloat16)
    weights = cell_weight.reshape(fronts, CELL_DEV, NNZ)
    pivots = cell_pivot.reshape(fronts, CELL_DEV, NNZ)

    def backward(inputs):
        factor, right, block, marks, index, weight, pivot = inputs
        values = sep_half[index] * marks[:, None]
        lifted = lax.dot_general(block.astype(jnp.float32), values.astype(jnp.float32), (((0,), (0,)), ((), ())), preferred_element_type=jnp.float32)
        potential = front_solve(factor, right - lifted)
        picked = potential[pivot]
        return jnp.sum(weight[:, :, None] * picked, axis=1).astype(jnp.bfloat16)
    field = lax.map(backward, (factors, rights, blocks, live_half, global_index, weights, pivots)).reshape(fronts * CELL_DEV, S)
    colfield = field.reshape(N_ROW, N_COL, CELL_DEV, S).transpose(1, 0, 2, 3).reshape(fronts * CELL_DEV, S)
    gram = lax.dot_general(field.astype(jnp.float32), colfield.astype(jnp.float32), (((1,), (1,)), ((), ())), preferred_element_type=jnp.float32) * (1.0 / S)
    return (sep_potential, gram * gram)
```

```python
import jax
import jax.numpy as jnp
from jax import lax
from jax.experimental import pallas as pl
from jax.experimental.pallas import tpu as pltpu
from jax.sharding import PartitionSpec as P

F32 = jnp.float32
BF16 = jnp.bfloat16
NN = (((1,), (0,)), ((), ()))
NT = (((1,), (1,)), ((), ()))
BASE = 256
PAD = 32
LANES = 128
VMEM = pltpu.VMEM
SMEM = pltpu.SMEM


def mm(a, b, dims=NN):
    return lax.dot_general(a, b, dims, preferred_element_type=F32)


def split(x):
    high = x.astype(BF16)
    return high, (x - high.astype(F32)).astype(BF16)


def mm3(a, b, dims=NN):
    return mm(a[0], b[0], dims) + (mm(a[0], b[1], dims) + mm(a[1], b[0], dims))


def invert_lower(blocks):
    order = blocks[0].shape[0]
    row = lax.broadcasted_iota(jnp.int32, (order, order), 0)
    col = lax.broadcasted_iota(jnp.int32, (order, order), 1)

    def below(level):
        same = (row >> (level + 1)) == (col >> (level + 1))
        return same & (((row >> level) & 1) == 1) & (((col >> level) & 1) == 0)

    found = []
    mask = below(0)
    for block in blocks:
        diagonal = jnp.where(row == col, block, 0.0)
        down = 1.0 / jnp.sum(diagonal, axis=1, keepdims=True)
        across = 1.0 / jnp.sum(diagonal, axis=0, keepdims=True)
        pairs = jnp.where(mask, -(down * block * across), 0.0)
        found.append(jnp.where(row == col, down, pairs))
    level = 1
    while (1 << level) < order:
        mask = below(level)
        parts = [split(one) for one in found]
        halves = [
            mm3(part, split(jnp.where(mask, block, 0.0))) for part, block in zip(parts, blocks)
        ]
        found = [one - mm3(split(half), part) for one, half, part in zip(found, halves, parts)]
        level += 1
    return found


def place_rows(source, target, owner_ref, count, slots, halves):
    width = source.shape[1]
    row = lax.broadcasted_iota(jnp.int32, (PAD, width), 0)
    for j in range(halves):
        rows = source[slots * j : slots * j + PAD, :]
        keep = (row < slots) & (row < count - slots * j)
        target[owner_ref[0, j]] = jnp.where(keep, rows, 0.0).astype(target.dtype)


def forward_kernel(
    owner_ref, count_ref, factor, rhs, coupling, out, high_out, low_out,
    diag, lower, right, block, high, low, contrib, sems,
):
    half = diag.shape[1]
    bound = coupling.shape[0]
    halves = owner_ref.shape[1]
    copies = [
        pltpu.make_async_copy(factor.at[0:half, 0:half], diag.at[0], sems.at[0]),
        pltpu.make_async_copy(factor.at[half : 2 * half, half : 2 * half], diag.at[1], sems.at[1]),
        pltpu.make_async_copy(rhs, right, sems.at[2]),
        pltpu.make_async_copy(factor.at[half : 2 * half, 0:half], lower, sems.at[3]),
        pltpu.make_async_copy(coupling, block, sems.at[4]),
    ]
    for copy in copies:
        copy.start()
    out[...] = jnp.zeros_like(out)
    contrib[bound:, :] = jnp.zeros((contrib.shape[0] - bound, contrib.shape[1]), F32)
    copies[0].wait()
    copies[1].wait()
    quarters = [
        diag[i, k * BASE : (k + 1) * BASE, k * BASE : (k + 1) * BASE]
        for i in range(2)
        for k in range(half // BASE)
    ]
    inverses = invert_lower(quarters)
    for i in range(2):
        first, second = inverses[2 * i], inverses[2 * i + 1]
        first_parts, second_parts = split(first), split(second)
        between = split(diag[i, BASE:, :BASE])
        corner = split(-mm3(second_parts, split(mm3(between, first_parts))))
        for k, ref in enumerate((high, low)):
            ref[i, :BASE, :BASE] = first_parts[k]
            ref[i, BASE:, BASE:] = second_parts[k]
            ref[i, BASE:, :BASE] = corner[k]
            ref[i, :BASE, BASE:] = jnp.zeros((BASE, BASE), BF16)
    keep = [
        pltpu.make_async_copy(high, high_out, sems.at[5]),
        pltpu.make_async_copy(low, low_out, sems.at[6]),
    ]
    for copy in keep:
        copy.start()
    copies[2].wait()
    copies[3].wait()
    inv = [(high[i], low[i]) for i in range(2)]
    off = split(lower[...])
    turned = right[...].T
    x0 = mm3(split(turned[:, :half]), inv[0], NT)
    x1 = mm3(split(turned[:, half:] - mm3(split(x0), off, NT)), inv[1], NT)
    y1 = mm3(split(x1), inv[1])
    y0 = mm3(split(x0 - mm3(split(y1), off)), inv[0])
    copies[4].wait()
    contrib[:bound, :] = mm(block[:, :half], y0.astype(BF16), NT) + mm(
        block[:, half:], y1.astype(BF16), NT
    )
    place_rows(contrib, out, owner_ref, count_ref[0], bound // halves, halves)
    for copy in keep:
        copy.wait()


def prepare_kernel(
    owner_ref, count_ref, factor, rhs, coupling, high, low, weight, pivot, sep,
    field0, g_high, g_low, s_high, s_low,
    lower, block, rows, placed, sems,
):
    half = lower.shape[0]
    bound = coupling.shape[0]
    halves = owner_ref.shape[1]
    cells = weight.shape[0]
    copies = [
        pltpu.make_async_copy(factor.at[half : 2 * half, 0:half], lower, sems.at[0]),
        pltpu.make_async_copy(coupling, block, sems.at[1]),
    ]
    for copy in copies:
        copy.start()
    first, second = invert_lower([sep[:BASE, :BASE], sep[BASE:, BASE:]])
    first_parts, second_parts = split(first), split(second)
    corner = -mm3(second_parts, split(mm3(split(sep[BASE:, :BASE]), first_parts)))
    corner_parts = split(corner)
    first_t, second_t, corner_t = split(first.T), split(second.T), split(corner.T)
    pieces = (
        (0, 0, mm3(first_t, first_parts) + mm3(corner_t, corner_parts)),
        (0, 1, mm3(corner_t, second_parts)),
        (1, 0, mm3(second_t, corner_parts)),
        (1, 1, mm3(second_t, second_parts)),
    )
    for i, k, piece in pieces:
        at = (slice(i * BASE, (i + 1) * BASE), slice(k * BASE, (k + 1) * BASE))
        s_high[at], s_low[at] = split(piece)

    places = lax.broadcasted_iota(jnp.int32, (cells, 2 * half), 1)
    project = jnp.zeros((cells, 2 * half), F32)
    for k in range(weight.shape[1]):
        project += jnp.where(places == pivot[:, k : k + 1], weight[:, k : k + 1], 0.0)
    copies[0].wait()
    inv = [(high[i], low[i]) for i in range(2)]
    off = split(lower[...])
    x0 = mm3(split(project[:, :half]), inv[0], NT)
    x1 = mm3(split(project[:, half:] - mm3(split(x0), off, NT)), inv[1], NT)
    y1 = mm3(split(x1), inv[1])
    y0 = mm3(split(x0 - mm3(split(y1), off)), inv[0])
    y0, y1 = split(y0), split(y1)
    field0[...] = mm3(y0, split(rhs[:half, :])) + mm3(y1, split(rhs[half:, :]))
    copies[1].wait()
    both = mm(block[:, :half], jnp.concatenate(y0, axis=0), NT) + mm(
        block[:, half:], jnp.concatenate(y1, axis=0), NT
    )
    rows[:bound, :] = both[:, :cells] + both[:, cells:]
    rows[bound:, :] = jnp.zeros((rows.shape[0] - bound, cells), F32)
    placed[...] = jnp.zeros_like(placed)
    place_rows(rows, placed, owner_ref, count_ref[0], bound // halves, halves)
    group = LANES // PAD
    for t in range(placed.shape[0] // group):
        tile = placed[t * group : (t + 1) * group].reshape(LANES, cells).T
        g_high[:, t * LANES : (t + 1) * LANES], g_low[:, t * LANES : (t + 1) * LANES] = split(tile)


def select_kernel(me_ref, index, sel, sel_t, *, bound, halves):
    fronts = index.shape[0]
    slots = bound // halves
    group = LANES // PAD
    me = me_ref[0]
    order = sel.shape[0]

    def one_hot(cond):
        return jnp.where(cond, 1.0, 0.0).astype(BF16)

    def owner_of(at):
        return (at * 2341) >> 16

    match = one_hot(index[:, bound : bound + halves] == me)
    spread = one_hot(
        owner_of(lax.broadcasted_iota(jnp.int32, (halves, bound), 1))
        == lax.broadcasted_iota(jnp.int32, (halves, bound), 0)
    )
    chosen = mm(match, spread)
    values = index[:, :bound]
    low = (chosen * (values & 255).astype(F32)).astype(BF16)
    high = (chosen * ((values >> 8) + 1).astype(F32)).astype(BF16)
    at = lax.broadcasted_iota(jnp.int32, (bound, LANES), 0)
    lane = lax.broadcasted_iota(jnp.int32, (bound, LANES), 1)
    fold = one_hot((at - slots * owner_of(at)) == (lane & (PAD - 1)))
    front = lax.broadcasted_iota(jnp.int32, (fronts, LANES), 0)
    part = lax.broadcasted_iota(jnp.int32, (fronts, LANES), 1) >> 5
    mine = (front & (group - 1)) == part
    low = jnp.where(mine, mm(low, fold), 0.0).astype(BF16)
    high = jnp.where(mine, mm(high, fold), 0.0).astype(BF16)
    groups = fronts // group
    gather = one_hot(
        (lax.broadcasted_iota(jnp.int32, (LANES, fronts), 1) >> 2)
        == lax.broadcasted_iota(jnp.int32, (LANES, fronts), 0)
    )
    flat = mm(gather, low) + 256.0 * (mm(gather, high) - 1.0)
    flat_t = flat.T
    flat = flat.astype(jnp.int32)
    flat_t = flat_t.astype(jnp.int32)
    down = lax.broadcasted_iota(jnp.int32, (order, LANES), 0)
    across = lax.broadcasted_iota(jnp.int32, (LANES, order), 1)
    for g in range(groups):
        sel[:, g * LANES : (g + 1) * LANES] = one_hot(down == flat[g : g + 1, :])
        sel_t[g * LANES : (g + 1) * LANES, :] = one_hot(across == flat_t[:, g : g + 1])


def separator_kernel(sel, incoming, sep_rhs, s_high, s_low, sel_t, potential, replies):
    reduced = sep_rhs[...] - mm(sel[...], incoming[...])
    found = mm3((s_high[...], s_low[...]), split(reduced))
    potential[...] = found
    replies[...] = mm(sel_t[...], found.astype(BF16)).astype(BF16)


def field_kernel(field0, g_high, g_low, returned, field):
    values = returned[...]
    field[...] = (field0[...] - (mm(g_high[...], values) + mm(g_low[...], values))).astype(BF16)


def call(kernel, outs, ins, scratch, specs, out_specs, flops, moved, vmem):
    return pl.pallas_call(
        kernel,
        out_shape=outs,
        in_specs=specs,
        out_specs=out_specs,
        scratch_shapes=scratch,
        compiler_params=pltpu.CompilerParams(vmem_limit_bytes=vmem * 1024 * 1024),
        cost_estimate=pl.CostEstimate(flops=flops, bytes_accessed=moved, transcendentals=0),
    )(*ins)


def local(
    rhs, front_factor, coupling, bound_count, sep_owner, sep_index, sep_rhs, sep_factor,
    cell_weight, cell_pivot,
):
    row_count = lax.axis_size("row")
    col_count = lax.axis_size("col")
    fronts = row_count * col_count
    bound, order = coupling.shape
    sources = rhs.shape[1]
    sep_size = sep_rhs.shape[0]
    halves = sep_owner.shape[1]
    cells = cell_weight.shape[0]
    half = order // 2
    flat = fronts * PAD
    vm = pl.BlockSpec(memory_space=VMEM)
    sm = pl.BlockSpec(memory_space=SMEM)
    hbm = pl.BlockSpec(memory_space=pl.ANY)
    shape = jax.ShapeDtypeStruct

    table = jnp.concatenate(
        [sep_index, sep_owner, jnp.zeros((1, 2048 - bound - halves), jnp.int32)], axis=1
    )
    every_index = lax.all_gather(table, ("row", "col"), axis=0, tiled=True)

    outgoing, inv_high, inv_low = call(
        forward_kernel,
        (
            shape((fronts, PAD, sources), BF16),
            shape((2, half, half), BF16),
            shape((2, half, half), BF16),
        ),
        (sep_owner, bound_count, front_factor, rhs, coupling),
        [
            VMEM((2, half, half), F32),
            VMEM((half, half), F32),
            VMEM((order, sources), F32),
            VMEM((bound, order), BF16),
            VMEM((2, half, half), BF16),
            VMEM((2, half, half), BF16),
            VMEM((bound + 8, sources), F32),
            pltpu.SemaphoreType.DMA((7,)),
        ],
        [sm, sm, hbm, hbm, hbm],
        (vm, hbm, hbm),
        8_000_000_000,
        14_000_000,
        40,
    )
    incoming = lax.all_to_all(outgoing, ("row", "col"), split_axis=0, concat_axis=0, tiled=True)
    field0, g_high, g_low, s_high, s_low = call(
        prepare_kernel,
        (
            shape((cells, sources), F32),
            shape((cells, flat), BF16),
            shape((cells, flat), BF16),
            shape((sep_size, sep_size), BF16),
            shape((sep_size, sep_size), BF16),
        ),
        (
            sep_owner, bound_count, front_factor, rhs, coupling, inv_high, inv_low,
            cell_weight, cell_pivot, sep_factor,
        ),
        [
            VMEM((half, half), F32),
            VMEM((bound, order), BF16),
            VMEM((bound + 8, cells), F32),
            VMEM((fronts, PAD, cells), F32),
            pltpu.SemaphoreType.DMA((2,)),
        ],
        [sm, sm, hbm, vm, hbm, vm, vm, vm, vm, vm],
        (vm,) * 5,
        6_000_000_000,
        14_000_000,
        40,
    )
    me = (lax.axis_index("row") * col_count + lax.axis_index("col")).astype(jnp.int32).reshape(1)
    sel, sel_t = call(
        lambda *refs: select_kernel(*refs, bound=bound, halves=halves),
        (shape((sep_size, flat), BF16), shape((flat, sep_size), BF16)),
        (me, every_index),
        [],
        [sm, vm],
        (vm, vm),
        1_000_000_000,
        9_000_000,
        24,
    )
    sep_potential, replies = call(
        separator_kernel,
        (shape((sep_size, sources), F32), shape((flat, sources), BF16)),
        (sel, incoming.reshape(flat, sources), sep_rhs, s_high, s_low, sel_t),
        [],
        [vm] * 6,
        (vm, vm),
        3_000_000_000,
        13_000_000,
        32,
    )
    returned = lax.all_to_all(
        replies.reshape(fronts, PAD, sources),
        ("row", "col"),
        split_axis=0,
        concat_axis=0,
        tiled=True,
    ).reshape(flat, sources)
    field = call(
        field_kernel,
        shape((cells, sources), BF16),
        (field0, g_high, g_low, returned),
        [],
        [vm] * 4,
        vm,
        600_000_000,
        5_000_000,
        16,
    )
    row_tile = lax.all_gather(field, "col", axis=0, tiled=True)
    col_tile = lax.all_to_all(
        jnp.broadcast_to(field[None], (row_count, cells, sources)),
        "row",
        split_axis=0,
        concat_axis=0,
        tiled=True,
    ).reshape(row_count * cells, sources)
    gram = mm(row_tile, col_tile, NT) * (1.0 / sources)
    return (sep_potential, gram * gram)


def solution(mesh):
    placed = P(("row", "col"), None)
    return jax.shard_map(
        local,
        mesh=mesh,
        in_specs=(placed, placed, placed, P(("row", "col"))) + (placed,) * 6,
        out_specs=(placed, P("row", "col")),
        check_vma=False,
    )
```

```python
import jax
import jax.numpy as jnp
from jax import lax
from jax.experimental import pallas as pl
from jax.experimental.pallas import tpu as pltpu
from jax.sharding import PartitionSpec as P

F32 = jnp.float32
BF16 = jnp.bfloat16
NN = (((1,), (0,)), ((), ()))
NT = (((1,), (1,)), ((), ()))
UNIT = 128
BASE = 256
WIDE = 512
PAD = 32
LANES = 128
VMEM = pltpu.VMEM
SMEM = pltpu.SMEM


def mm(a, b, dims=NN):
    return lax.dot_general(a, b, dims, preferred_element_type=F32)


def split(x):
    high = x.astype(BF16)
    return high, (x - high.astype(F32)).astype(BF16)


def mm3(a, b, dims=NN):
    return mm(a[0], b[0], dims) + (mm(a[0], b[1], dims) + mm(a[1], b[0], dims))


def side_by_side(first, second):
    return jnp.concatenate([first, second], axis=1)


def on_diagonal(pair):
    order = pair.shape[0]
    zero = jnp.zeros((order, order), pair.dtype)
    return jnp.concatenate(
        [side_by_side(pair[:, :order], zero), side_by_side(zero, pair[:, order:])], axis=0
    )


def mm_pair(a, b):
    return mm3(a, (on_diagonal(b[0]), on_diagonal(b[1])))


def invert_lower(read, count):
    row = lax.broadcasted_iota(jnp.int32, (UNIT, 2 * UNIT), 0)
    col = lax.broadcasted_iota(jnp.int32, (UNIT, 2 * UNIT), 1) & (UNIT - 1)
    first = lax.broadcasted_iota(jnp.int32, (UNIT, 2 * UNIT), 1) < UNIT

    def below(level):
        same = (row >> (level + 1)) == (col >> (level + 1))
        return same & (((row >> level) & 1) == 1) & (((col >> level) & 1) == 0)

    pairs = [side_by_side(read(b, 0, 0), read(b, 1, 1)) for b in range(count)]
    found = []
    mask = below(0)
    for pair in pairs:
        diagonal = jnp.where(row == col, pair, 0.0)
        across = 1.0 / jnp.where(row == col, pair, 1.0)
        across = jnp.sum(jnp.where(row == col, across, 0.0), axis=0, keepdims=True)
        down = 1.0 / jnp.where(
            first,
            jnp.sum(diagonal[:, :UNIT], axis=1, keepdims=True),
            jnp.sum(diagonal[:, UNIT:], axis=1, keepdims=True),
        )
        below_it = jnp.where(mask, -(down * pair * across), 0.0)
        found.append(jnp.where(row == col, down, below_it))
    level = 1
    while (1 << level) < UNIT:
        mask = below(level)
        parts = [split(one) for one in found]
        halves = [mm_pair(p, split(jnp.where(mask, pair, 0.0))) for p, pair in zip(parts, pairs)]
        found = [one - mm_pair(split(h), p) for one, h, p in zip(found, halves, parts)]
        level += 1
    result = []
    for b in range(0, count, 2):
        left, right = found[b], found[b + 1]
        tops = split(side_by_side(left[:, :UNIT], right[:, :UNIT]))
        ends = split(side_by_side(left[:, UNIT:], right[:, UNIT:]))
        between = split(side_by_side(read(b, 1, 0), read(b + 1, 1, 0)))
        corners = -mm_pair(ends, split(mm_pair(between, tops)))
        zero = jnp.zeros((UNIT, UNIT), F32)
        for k, one in enumerate((left, right)):
            corner = corners[:, k * UNIT : (k + 1) * UNIT]
            result.append(
                jnp.concatenate(
                    [side_by_side(one[:, :UNIT], zero), side_by_side(corner, one[:, UNIT:])], axis=0
                )
            )
    return result


def place_rows(source, target, owner_ref, count, slots, halves, extra=None):
    width = target.shape[2]
    row = lax.broadcasted_iota(jnp.int32, (PAD, width), 0)
    for j in range(halves):
        live = jnp.minimum(count - slots * j, slots)
        rows = source[slots * j : slots * j + PAD, :]
        rows = jnp.where(row < live, rows, 0.0)
        if extra is not None:
            rows = jnp.where(row == slots, extra[j : j + 1, :], rows)
        target[owner_ref[0, j]] = rows.astype(target.dtype)


def one_hot(cond):
    return jnp.where(cond, 1.0, 0.0).astype(BF16)


def group_of(row):
    return (row * 2341) >> 16


def forward_kernel(
    owner_ref, count_ref, me_ref, index, factor, rhs, coupling,
    out_hbm, high_out, low_out,
    diag, lower, right, block, high, low, contrib, out, sems,
):
    half = diag.shape[1]
    bound = coupling.shape[0]
    halves = owner_ref.shape[1]
    slots = bound // halves
    copies = [
        pltpu.make_async_copy(factor.at[0:half, 0:half], diag.at[0], sems.at[0]),
        pltpu.make_async_copy(factor.at[half : 2 * half, half : 2 * half], diag.at[1], sems.at[1]),
        pltpu.make_async_copy(rhs, right, sems.at[2]),
        pltpu.make_async_copy(factor.at[half : 2 * half, 0:half], lower, sems.at[3]),
        pltpu.make_async_copy(coupling, block, sems.at[4]),
    ]
    for copy in copies:
        copy.start()
    out[...] = jnp.zeros_like(out)
    contrib[bound:, :] = jnp.zeros((contrib.shape[0] - bound, contrib.shape[1]), F32)
    mine = group_of(lax.broadcasted_iota(jnp.int32, (halves, bound), 1)) == (
        lax.broadcasted_iota(jnp.int32, (halves, bound), 0)
    )
    values = index[...]
    low_bits = jnp.where(mine, (values & 255).astype(F32), 0.0).astype(BF16)
    high_bits = jnp.where(mine, ((values >> 8) + 1).astype(F32), 0.0).astype(BF16)
    at = lax.broadcasted_iota(jnp.int32, (bound, LANES), 0)
    lane = lax.broadcasted_iota(jnp.int32, (bound, LANES), 1)
    part = me_ref[0] & (LANES // PAD - 1)
    fold = one_hot((at - slots * group_of(at)) + PAD * part == lane)
    extra = side_by_side(mm(low_bits, fold), mm(high_bits, fold))
    copies[0].wait()
    copies[1].wait()

    def read(b, i, k):
        top = (b % 2) * BASE
        return diag[
            b // 2, top + i * UNIT : top + (i + 1) * UNIT, top + k * UNIT : top + (k + 1) * UNIT
        ]

    inverses = invert_lower(read, 4)
    for i in range(2):
        first_parts, second_parts = split(inverses[2 * i]), split(inverses[2 * i + 1])
        between = split(diag[i, BASE:, :BASE])
        corner = split(-mm3(second_parts, split(mm3(between, first_parts))))
        for k, ref in enumerate((high, low)):
            ref[i, :BASE, :BASE] = first_parts[k]
            ref[i, BASE:, BASE:] = second_parts[k]
            ref[i, BASE:, :BASE] = corner[k]
            ref[i, :BASE, BASE:] = jnp.zeros((BASE, BASE), BF16)
    keep = [
        pltpu.make_async_copy(high, high_out, sems.at[5]),
        pltpu.make_async_copy(low, low_out, sems.at[6]),
    ]
    for copy in keep:
        copy.start()
    copies[2].wait()
    copies[3].wait()
    inv = [(high[i], low[i]) for i in range(2)]
    off = split(lower[...])
    turned = right[...].T
    x0 = mm3(split(turned[:, :half]), inv[0], NT)
    x1 = mm3(split(turned[:, half:] - mm3(split(x0), off, NT)), inv[1], NT)
    y1 = mm3(split(x1), inv[1])
    y0 = mm3(split(x0 - mm3(split(y1), off)), inv[0])
    copies[4].wait()
    contrib[:bound, :] = mm(block[:, :half], y0.astype(BF16), NT) + mm(
        block[:, half:], y1.astype(BF16), NT
    )
    place_rows(contrib, out, owner_ref, count_ref[0], slots, halves, extra)
    keep.append(pltpu.make_async_copy(out, out_hbm, sems.at[0]))
    keep[-1].start()
    for copy in keep:
        copy.wait()


def schur_kernel(sep_hbm, s_high, s_low, sep, sem):
    copy = pltpu.make_async_copy(sep_hbm, sep, sem)
    copy.start()
    copy.wait()

    def read(b, i, k):
        top = b * BASE
        return sep[top + i * UNIT : top + (i + 1) * UNIT, top + k * UNIT : top + (k + 1) * UNIT]

    first, second = invert_lower(read, 2)
    first_parts, second_parts = split(first), split(second)
    corner = -mm3(second_parts, split(mm3(split(sep[BASE:, :BASE]), first_parts)))
    corner_parts = split(corner)
    first_t, second_t, corner_t = split(first.T), split(second.T), split(corner.T)
    pieces = (
        (0, 0, mm3(first_t, first_parts) + mm3(corner_t, corner_parts)),
        (0, 1, mm3(corner_t, second_parts)),
        (1, 0, mm3(second_t, corner_parts)),
        (1, 1, mm3(second_t, second_parts)),
    )
    for i, k, piece in pieces:
        at = (slice(i * BASE, (i + 1) * BASE), slice(k * BASE, (k + 1) * BASE))
        s_high[at], s_low[at] = split(piece)


def project_kernel(
    owner_ref, count_ref, factor, rhs, coupling, high_hbm, low_hbm, weight, pivot,
    field0, g_high, g_low,
    lower, right, block, high, low, rows, placed, sems,
):
    half = lower.shape[0]
    bound = coupling.shape[0]
    halves = owner_ref.shape[1]
    cells = weight.shape[0]
    copies = [
        pltpu.make_async_copy(high_hbm, high, sems.at[0]),
        pltpu.make_async_copy(low_hbm, low, sems.at[1]),
        pltpu.make_async_copy(factor.at[half : 2 * half, 0:half], lower, sems.at[2]),
        pltpu.make_async_copy(rhs, right, sems.at[3]),
        pltpu.make_async_copy(coupling, block, sems.at[4]),
    ]
    for copy in copies:
        copy.start()
    placed[...] = jnp.zeros_like(placed)
    places = lax.broadcasted_iota(jnp.int32, (cells, 2 * half), 1)
    project = jnp.zeros((cells, 2 * half), F32)
    for k in range(weight.shape[1]):
        project += jnp.where(places == pivot[:, k : k + 1], weight[:, k : k + 1], 0.0)
    for copy in copies[:3]:
        copy.wait()
    inv = [(high[i], low[i]) for i in range(2)]
    off = split(lower[...])
    x0 = mm3(split(project[:, :half]), inv[0], NT)
    x1 = mm3(split(project[:, half:] - mm3(split(x0), off, NT)), inv[1], NT)
    y1 = mm3(split(x1), inv[1])
    y0 = mm3(split(x0 - mm3(split(y1), off)), inv[0])
    y0, y1 = split(y0), split(y1)
    copies[3].wait()
    field0[...] = mm3(y0, split(right[:half, :])) + mm3(y1, split(right[half:, :]))
    copies[4].wait()
    both = mm(block[:, :half], jnp.concatenate(y0, axis=0), NT) + mm(
        block[:, half:], jnp.concatenate(y1, axis=0), NT
    )
    rows[:bound, :] = both[:, :cells] + both[:, cells:]
    rows[bound:, :] = jnp.zeros((rows.shape[0] - bound, cells), F32)
    place_rows(rows, placed, owner_ref, count_ref[0], bound // halves, halves)
    group = LANES // PAD
    for t in range(placed.shape[0] // group):
        tile = placed[t * group : (t + 1) * group].reshape(LANES, cells).T
        g_high[:, t * LANES : (t + 1) * LANES], g_low[:, t * LANES : (t + 1) * LANES] = split(tile)


def pick(cond):
    return jnp.where(cond, jnp.ones((), BF16), jnp.zeros((), BF16))


def separator_kernel(
    incoming, rhs_hbm, high_hbm, low_hbm, potential, replies, right, high, low, sems, *, fronts, slots
):
    copies = [
        pltpu.make_async_copy(source, target, sems.at[k])
        for k, (source, target) in enumerate(((rhs_hbm, right), (high_hbm, high), (low_hbm, low)))
    ]
    for copy in copies:
        copy.start()
    group = LANES // PAD
    tail = incoming[...].reshape(fronts, PAD, -1)[:, PAD - 8 :, :].astype(F32)
    tail = tail.reshape(fronts // group, group, 8, -1)
    tail = (tail[:, 0] + tail[:, 1]) + (tail[:, 2] + tail[:, 3])
    tail = tail[:, slots - (PAD - 8), :]
    low_bits, high_bits = tail[:, :LANES], tail[:, LANES:]
    rows = [jnp.where(high_bits == 1.0 + p, low_bits, -1.0) for p in range(2)]
    empty = jnp.full((LANES - rows[0].shape[0], LANES), -1.0, F32)
    cols = [jnp.concatenate([one, empty], axis=0).T for one in rows]
    part = right.shape[0] // 2
    down = lax.broadcasted_iota(jnp.int32, (part, LANES), 0).astype(F32).astype(BF16)
    along = lax.broadcasted_iota(jnp.int32, (LANES, part), 1).astype(F32).astype(BF16)
    groups = incoming.shape[0] // LANES
    each = WIDE // LANES
    total = None
    for c in range(groups // each):
        tiles = [
            jnp.concatenate(
                [pick(down == rows[p][g : g + 1, :].astype(BF16)) for p in range(2)], axis=0
            )
            for g in range(c * each, (c + 1) * each)
        ]
        term = mm(jnp.concatenate(tiles, axis=1), incoming[c * WIDE : (c + 1) * WIDE, :])
        total = term if total is None else total + term
    for copy in copies:
        copy.wait()
    found = mm3((high[...], low[...]), split(right[...] - total))
    potential[...] = found
    rounded = found.astype(BF16)
    for c in range(groups // each):
        tiles = [
            jnp.concatenate(
                [pick(along == cols[p][:, g : g + 1].astype(BF16)) for p in range(2)], axis=1
            )
            for g in range(c * each, (c + 1) * each)
        ]
        chosen = jnp.concatenate(tiles, axis=0)
        replies[c * WIDE : (c + 1) * WIDE, :] = mm(chosen, rounded).astype(BF16)


def field_kernel(field0, g_high, g_low, returned, field, spread):
    values = returned[...]
    found = (field0[...] - (mm(g_high[...], values) + mm(g_low[...], values))).astype(BF16)
    field[...] = found
    for r in range(spread.shape[0]):
        spread[r] = found


def hess_kernel(me_ref, pair, *refs):
    others, col_tile, hess = refs[:-5], refs[-5], refs[-4]
    row_tile, tiles, sems = refs[-3:]
    scale = 1.0 / col_tile.shape[1]
    me = me_ref[0]
    for d, block in enumerate((pair,) + others):
        row_tile[me ^ (2 * d)] = block[0]
        row_tile[me ^ (2 * d + 1)] = block[1]
    rows = row_tile[...].reshape(-1, col_tile.shape[1])
    slots, _, width = tiles.shape
    copies = []
    for t in range(hess.shape[1] // width):
        slot = t % slots
        if t >= slots:
            copies[t - slots].wait()
        gram = mm(rows, col_tile[t * width : (t + 1) * width, :], NT) * scale
        tiles[slot] = gram * gram
        copies.append(
            pltpu.make_async_copy(
                tiles.at[slot], hess.at[:, t * width : (t + 1) * width], sems.at[slot]
            )
        )
        copies[-1].start()
    for copy in copies[-slots:]:
        copy.wait()


def call(kernel, outs, ins, scratch, specs, out_specs, flops, moved, vmem):
    return pl.pallas_call(
        kernel,
        out_shape=outs,
        in_specs=specs,
        out_specs=out_specs,
        scratch_shapes=scratch,
        compiler_params=pltpu.CompilerParams(vmem_limit_bytes=vmem * 1024 * 1024),
        cost_estimate=pl.CostEstimate(flops=flops, bytes_accessed=moved, transcendentals=0),
    )(*ins)


def local(
    rhs, front_factor, coupling, bound_count, sep_owner, sep_index, sep_rhs, sep_factor,
    cell_weight, cell_pivot,
):
    row_count = lax.axis_size("row")
    col_count = lax.axis_size("col")
    fronts = row_count * col_count
    bound, order = coupling.shape
    sources = rhs.shape[1]
    sep_size = sep_rhs.shape[0]
    halves = sep_owner.shape[1]
    cells = cell_weight.shape[0]
    half = order // 2
    flat = fronts * PAD
    vm = pl.BlockSpec(memory_space=VMEM)
    sm = pl.BlockSpec(memory_space=SMEM)
    hbm = pl.BlockSpec(memory_space=pl.ANY)
    shape = jax.ShapeDtypeStruct

    dma = pltpu.SemaphoreType.DMA
    both = ("row", "col")
    me = lax.axis_index("col").astype(jnp.int32).reshape(1)
    outgoing, inv_high, inv_low = call(
        forward_kernel,
        (
            shape((fronts, PAD, sources), BF16),
            shape((2, half, half), BF16),
            shape((2, half, half), BF16),
        ),
        (sep_owner, bound_count, me, sep_index, front_factor, rhs, coupling),
        [
            VMEM((2, half, half), F32),
            VMEM((half, half), F32),
            VMEM((order, sources), F32),
            VMEM((bound, order), BF16),
            VMEM((2, half, half), BF16),
            VMEM((2, half, half), BF16),
            VMEM((bound + 8, sources), F32),
            VMEM((fronts, PAD, sources), BF16),
            dma((7,)),
        ],
        [sm, sm, sm, vm, hbm, hbm, hbm],
        (hbm,) * 3,
        8_000_000_000,
        14_000_000,
        58,
    )

    def exchange(blocks):
        return lax.all_to_all(
            blocks.reshape(fronts, PAD, sources), both, split_axis=0, concat_axis=0, tiled=True
        ).reshape(flat, sources)

    incoming = exchange(outgoing)
    s_high, s_low = call(
        schur_kernel,
        (shape((sep_size, sep_size), BF16), shape((sep_size, sep_size), BF16)),
        (sep_factor,),
        [VMEM((sep_size, sep_size), F32), dma],
        [hbm],
        (vm, vm),
        2_000_000_000,
        3_000_000,
        24,
    )
    sep_potential, replies = call(
        lambda *refs: separator_kernel(*refs, fronts=fronts, slots=bound // halves),
        (shape((sep_size, sources), F32), shape((flat, sources), BF16)),
        (incoming, sep_rhs, s_high, s_low),
        [
            VMEM((sep_size, sources), F32),
            VMEM((sep_size, sep_size), BF16),
            VMEM((sep_size, sep_size), BF16),
            dma((3,)),
        ],
        [vm, hbm, hbm, hbm],
        (vm, vm),
        3_000_000_000,
        5_000_000,
        28,
    )
    returned = exchange(replies)
    weight, _ = lax.optimization_barrier((cell_weight, sep_potential))
    field0, g_high, g_low = call(
        project_kernel,
        (
            shape((cells, sources), F32),
            shape((cells, flat), BF16),
            shape((cells, flat), BF16),
        ),
        (
            sep_owner, bound_count, front_factor, rhs, coupling, inv_high, inv_low,
            weight, cell_pivot,
        ),
        [
            VMEM((half, half), F32),
            VMEM((order, sources), F32),
            VMEM((bound, order), BF16),
            VMEM((2, half, half), BF16),
            VMEM((2, half, half), BF16),
            VMEM((bound + 8, cells), F32),
            VMEM((fronts, PAD, cells), F32),
            dma((5,)),
        ],
        [sm, sm, hbm, hbm, hbm, hbm, hbm, vm, vm],
        (vm,) * 3,
        4_000_000_000,
        11_000_000,
        32,
    )
    field, spread = call(
        field_kernel,
        (shape((cells, sources), BF16), shape((row_count, cells, sources), BF16)),
        (field0, g_high, g_low, returned),
        [],
        [vm] * 4,
        (vm, vm),
        600_000_000,
        5_000_000,
        16,
    )
    col_tile = lax.all_to_all(
        spread, "row", split_axis=0, concat_axis=0, tiled=True
    ).reshape(row_count * cells, sources)
    mate = lax.ppermute(field, "col", [(i, i ^ 1) for i in range(col_count)])
    pair = jnp.stack([field, mate])
    others = [
        lax.ppermute(pair, "col", [(i, i ^ (2 * d)) for i in range(col_count)])
        for d in range(1, col_count // 2)
    ]
    hess = call(
        hess_kernel,
        shape((col_count * cells, row_count * cells), F32),
        (me, pair, *others, col_tile),
        [
            VMEM((col_count, cells, sources), BF16),
            VMEM((4, col_count * cells, BASE), F32),
            dma((4,)),
        ],
        [sm] + [vm] * (col_count // 2 + 1),
        hbm,
        1_000_000_000,
        10_000_000,
        24,
    )
    return (sep_potential, hess)


def solution(mesh):
    placed = P(("row", "col"), None)
    return jax.shard_map(
        local,
        mesh=mesh,
        in_specs=(placed, placed, placed, P(("row", "col"))) + (placed,) * 6,
        out_specs=(placed, P("row", "col")),
        check_vma=False,
    )
```

```python
import jax
import jax.numpy as jnp
from jax import lax
from jax.experimental import pallas as pl
from jax.experimental.pallas import tpu as pltpu
from jax.sharding import PartitionSpec as P

F32 = jnp.float32
BF16 = jnp.bfloat16
NN = (((1,), (0,)), ((), ()))
NT = (((1,), (1,)), ((), ()))
UNIT = 128
BASE = 256
WIDE = 512
FULL = 60.5
PAD = 32
LANES = 128
VMEM = pltpu.VMEM
SMEM = pltpu.SMEM


def mm(a, b, dims=NN):
    return lax.dot_general(a, b, dims, preferred_element_type=F32)


def split(x):
    high = x.astype(BF16)
    return high, (x - high.astype(F32)).astype(BF16)


def mm3(a, b, dims=NN):
    return mm(a[0], b[0], dims) + (mm(a[0], b[1], dims) + mm(a[1], b[0], dims))


def side_by_side(first, second):
    return jnp.concatenate([first, second], axis=1)


def on_diagonal(pair):
    order = pair.shape[0]
    zero = jnp.zeros((order, order), pair.dtype)
    return jnp.concatenate(
        [side_by_side(pair[:, :order], zero), side_by_side(zero, pair[:, order:])], axis=0
    )


def mm_pair(a, b):
    return mm3(a, (on_diagonal(b[0]), on_diagonal(b[1])))


def invert_lower(read, count, midway=None):
    row = lax.broadcasted_iota(jnp.int32, (UNIT, 2 * UNIT), 0)
    col = lax.broadcasted_iota(jnp.int32, (UNIT, 2 * UNIT), 1) & (UNIT - 1)
    first = lax.broadcasted_iota(jnp.int32, (UNIT, 2 * UNIT), 1) < UNIT

    def below(level):
        same = (row >> (level + 1)) == (col >> (level + 1))
        return same & (((row >> level) & 1) == 1) & (((col >> level) & 1) == 0)

    pairs = [side_by_side(read(b, 0, 0), read(b, 1, 1)) for b in range(count)]
    found = []
    mask = below(0)
    for pair in pairs:
        diagonal = jnp.where(row == col, pair, 0.0)
        across = 1.0 / jnp.where(row == col, pair, 1.0)
        across = jnp.sum(jnp.where(row == col, across, 0.0), axis=0, keepdims=True)
        down = 1.0 / jnp.where(
            first,
            jnp.sum(diagonal[:, :UNIT], axis=1, keepdims=True),
            jnp.sum(diagonal[:, UNIT:], axis=1, keepdims=True),
        )
        below_it = jnp.where(mask, -(down * pair * across), 0.0)
        found.append(jnp.where(row == col, down, below_it))
    level = 1
    while (1 << level) < UNIT:
        if level == 3 and midway is not None:
            midway()
        mask = below(level)
        parts = [split(one) for one in found]
        halves = [mm_pair(p, split(jnp.where(mask, pair, 0.0))) for p, pair in zip(parts, pairs)]
        found = [one - mm_pair(split(h), p) for one, h, p in zip(found, halves, parts)]
        level += 1
    result = []
    for b in range(0, count, 2):
        left, right = found[b], found[b + 1]
        tops = split(side_by_side(left[:, :UNIT], right[:, :UNIT]))
        ends = split(side_by_side(left[:, UNIT:], right[:, UNIT:]))
        between = split(side_by_side(read(b, 1, 0), read(b + 1, 1, 0)))
        corners = -mm_pair(ends, split(mm_pair(between, tops)))
        zero = jnp.zeros((UNIT, UNIT), F32)
        for k, one in enumerate((left, right)):
            corner = corners[:, k * UNIT : (k + 1) * UNIT]
            result.append(
                jnp.concatenate(
                    [side_by_side(one[:, :UNIT], zero), side_by_side(corner, one[:, UNIT:])], axis=0
                )
            )
    return result


def solve_rows(rows, high, low, off):
    half = off[0].shape[0]
    inv = [(high[i], low[i]) for i in range(2)]
    x0 = mm3(split(rows[:, :half]), inv[0], NT)
    x1 = mm3(split(rows[:, half:] - mm3(split(x0), off, NT)), inv[1], NT)
    y1 = mm3(split(x1), inv[1])
    y0 = mm3(split(x0 - mm3(split(y1), off)), inv[0])
    return y0, y1


def copy_all(pairs, sems, first=0):
    return [
        pltpu.make_async_copy(source, target, sems.at[first + k])
        for k, (source, target) in enumerate(pairs)
    ]


def start(copies):
    for copy in copies:
        copy.start()


def wait(copies):
    for copy in copies:
        copy.wait()


def place_rows(source, target, owner_ref, count, slots, halves, extra=None):
    width = target.shape[2]
    row = lax.broadcasted_iota(jnp.int32, (PAD, width), 0)
    for j in range(halves):
        live = jnp.minimum(count - slots * j, slots)
        rows = source[slots * j : slots * j + PAD, :]
        rows = jnp.where(row < live, rows, 0.0)
        if extra is not None:
            rows = jnp.where(row == slots, extra[j : j + 1, :], rows)
        target[owner_ref[0, j]] = rows.astype(target.dtype)


def one_hot(cond):
    return jnp.where(cond, 1.0, 0.0).astype(BF16)


def group_of(row):
    return (row * 2341) >> 16


def forward_kernel(
    owner_ref, count_ref, me_ref, index, factor, rhs, coupling,
    out_hbm, high_out, low_out,
    diag, between, lower, right, block, high, low, contrib, out, sems,
):
    quarters = diag.shape[0]
    half = lower.shape[0]
    bound = coupling.shape[0]
    halves = owner_ref.shape[1]
    slots = bound // halves
    pieces = 4

    def tile(i, k):
        return factor.at[i * BASE : (i + 1) * BASE, k * BASE : (k + 1) * BASE]

    factor_copies = copy_all([(tile(k, k), diag.at[k]) for k in range(quarters)], sems)
    rest_copies = copy_all(
        [(tile(2 * i + 1, 2 * i), between.at[i]) for i in range(2)]
        + [(rhs, right), (factor.at[half : 2 * half, 0:half], lower), (coupling, block)],
        sems,
        quarters,
    )
    start(factor_copies + rest_copies)
    out[...] = jnp.zeros_like(out)
    contrib[bound:, :] = jnp.zeros((contrib.shape[0] - bound, contrib.shape[1]), F32)
    mine = group_of(lax.broadcasted_iota(jnp.int32, (halves, bound), 1)) == (
        lax.broadcasted_iota(jnp.int32, (halves, bound), 0)
    )
    values = index[...]
    low_bits = jnp.where(mine, (values & 255).astype(F32), 0.0).astype(BF16)
    high_bits = jnp.where(mine, ((values >> 8) + 1).astype(F32), 0.0).astype(BF16)
    at = lax.broadcasted_iota(jnp.int32, (bound, LANES), 0)
    lane = lax.broadcasted_iota(jnp.int32, (bound, LANES), 1)
    part = me_ref[0] & (LANES // PAD - 1)
    fold = one_hot((at - slots * group_of(at)) + PAD * part == lane)
    extra = side_by_side(mm(low_bits, fold), mm(high_bits, fold))
    wait(factor_copies)

    def read(b, i, k):
        return diag[b, i * UNIT : (i + 1) * UNIT, k * UNIT : (k + 1) * UNIT]

    sides = []

    def midway():
        wait(rest_copies[:4])
        sides.extend((right[...].T, split(lower[...])))

    inverses = invert_lower(read, quarters, midway)
    for i in range(2):
        first_parts, second_parts = split(inverses[2 * i]), split(inverses[2 * i + 1])
        corner = split(-mm3(second_parts, split(mm3(split(between[i]), first_parts))))
        for k, ref in enumerate((high, low)):
            ref[i, :BASE, :BASE] = first_parts[k]
            ref[i, BASE:, BASE:] = second_parts[k]
            ref[i, BASE:, :BASE] = corner[k]
            ref[i, :BASE, BASE:] = jnp.zeros((BASE, BASE), BF16)
    keep = copy_all([(high, high_out), (low, low_out)], sems)
    start(keep)
    y0, y1 = solve_rows(sides[0], high, low, sides[1])
    wait(rest_copies[4:])
    contrib[:bound, :] = mm(block[:, :half], y0.astype(BF16), NT) + mm(
        block[:, half:], y1.astype(BF16), NT
    )
    place_rows(contrib, out, owner_ref, count_ref[0], slots, halves, extra)
    size = out.shape[0] // pieces
    send = copy_all(
        [
            (out.at[k * size : (k + 1) * size], out_hbm.at[k * size : (k + 1) * size])
            for k in range(pieces)
        ],
        sems,
        quarters,
    )
    start(send)
    wait(keep)
    wait(send)


def schur_kernel(sep_hbm, rhs_hbm, both, sep, sems):
    order = sep.shape[0]
    copies = copy_all([(sep_hbm, sep), (rhs_hbm, both.at[:, order:])], sems)
    start(copies)
    copies[0].wait()

    def read(b, i, k):
        top = b * BASE
        return sep[top + i * UNIT : top + (i + 1) * UNIT, top + k * UNIT : top + (k + 1) * UNIT]

    first, second = invert_lower(read, 2)
    first_parts, second_parts = split(first), split(second)
    corner = -mm3(second_parts, split(mm3(split(sep[BASE:, :BASE]), first_parts)))
    corner_parts = split(corner)
    first_t, second_t, corner_t = split(first.T), split(second.T), split(corner.T)
    pieces = (
        (0, 0, mm3(first_t, first_parts) + mm3(corner_t, corner_parts)),
        (0, 1, mm3(corner_t, second_parts)),
        (1, 0, mm3(second_t, corner_parts)),
        (1, 1, mm3(second_t, second_parts)),
    )
    for i, k, piece in pieces:
        at = (slice(i * BASE, (i + 1) * BASE), slice(k * BASE, (k + 1) * BASE))
        both[at] = piece
    copies[1].wait()


def project_kernel(
    owner_ref, count_ref, factor, rhs, coupling, high_hbm, low_hbm, weight, pivot,
    field0, g_high, g_low,
    lower, right, block, high, low, rows, placed, sems,
):
    half = lower.shape[0]
    bound = coupling.shape[0]
    halves = owner_ref.shape[1]
    cells = weight.shape[0]
    copies = [
        pltpu.make_async_copy(high_hbm, high, sems.at[0]),
        pltpu.make_async_copy(low_hbm, low, sems.at[1]),
        pltpu.make_async_copy(factor.at[half : 2 * half, 0:half], lower, sems.at[2]),
        pltpu.make_async_copy(rhs, right, sems.at[3]),
        pltpu.make_async_copy(coupling, block, sems.at[4]),
    ]
    for copy in copies:
        copy.start()
    placed[...] = jnp.zeros_like(placed)
    places = lax.broadcasted_iota(jnp.int32, (cells, 2 * half), 1)
    project = jnp.zeros((cells, 2 * half), F32)
    for k in range(weight.shape[1]):
        project += jnp.where(places == pivot[:, k : k + 1], weight[:, k : k + 1], 0.0)
    for copy in copies[:3]:
        copy.wait()
    y0, y1 = solve_rows(project, high, low, split(lower[...]))
    y0, y1 = split(y0), split(y1)
    copies[3].wait()
    field0[...] = mm3(y0, split(right[:half, :])) + mm3(y1, split(right[half:, :]))
    copies[4].wait()
    both = mm(block[:, :half], jnp.concatenate(y0, axis=0), NT) + mm(
        block[:, half:], jnp.concatenate(y1, axis=0), NT
    )
    rows[:bound, :] = both[:, :cells] + both[:, cells:]
    rows[bound:, :] = jnp.zeros((rows.shape[0] - bound, cells), F32)
    place_rows(rows, placed, owner_ref, count_ref[0], bound // halves, halves)
    group = LANES // PAD
    for t in range(placed.shape[0] // group):
        tile = placed[t * group : (t + 1) * group].reshape(LANES, cells).T
        g_high[:, t * LANES : (t + 1) * LANES], g_low[:, t * LANES : (t + 1) * LANES] = split(tile)


def pick(cond):
    return jnp.where(cond, jnp.ones((), BF16), jnp.zeros((), BF16))


def separator_kernel(
    incoming, schur_hbm, potential_hbm, replies_hbm, schur, potential, replies, sems, *, slots
):
    fronts = incoming.shape[0]
    chunks = fronts * PAD // WIDE
    per = WIDE // PAD
    rest = copy_all([(schur_hbm, schur)], sems)
    start(rest)
    group = LANES // PAD
    tail = incoming[:, PAD - 8 :, :].astype(F32)
    tail = tail.reshape(fronts // group, group, 8, -1)
    tail = (tail[:, 0] + tail[:, 1]) + (tail[:, 2] + tail[:, 3])
    tail = tail[:, slots - (PAD - 8), :]
    low_bits, high_bits = tail[:, :LANES], tail[:, LANES:]
    rows = [jnp.where(high_bits == 1.0 + p, low_bits, -1.0) for p in range(2)]
    empty = jnp.full((LANES - rows[0].shape[0], LANES), -1.0, F32)
    cols = [jnp.concatenate([one, empty], axis=0).T for one in rows]
    order = schur.shape[0]
    part = order // 2
    down = lax.broadcasted_iota(jnp.int32, (part, LANES), 0).astype(F32).astype(BF16)
    along = lax.broadcasted_iota(jnp.int32, (LANES, part), 1).astype(F32).astype(BF16)
    each = WIDE // LANES
    total = None
    for c in range(chunks):
        tiles = [
            jnp.concatenate(
                [pick(down == rows[p][g : g + 1, :].astype(BF16)) for p in range(2)], axis=0
            )
            for g in range(c * each, (c + 1) * each)
        ]
        values = incoming[c * per : (c + 1) * per].reshape(WIDE, -1)
        term = mm(jnp.concatenate(tiles, axis=1), values)
        total = term if total is None else total + term
    wait(rest)
    found = mm3(split(schur[:, :order]), split(schur[:, order:] - total))
    potential[...] = found
    stores = copy_all([(potential, potential_hbm)], sems)
    start(stores)
    rounded = found.astype(BF16)
    for c in range(chunks):
        tiles = [
            jnp.concatenate(
                [pick(along == cols[p][:, g : g + 1].astype(BF16)) for p in range(2)], axis=1
            )
            for g in range(c * each, (c + 1) * each)
        ]
        chosen = jnp.concatenate(tiles, axis=0)
        replies[c * per : (c + 1) * per] = (
            mm(chosen, rounded).astype(BF16).reshape(per, PAD, rounded.shape[1])
        )
        if (c + 1) % (chunks // 2) == 0:
            first = (c + 1 - chunks // 2) * per
            last = (c + 1) * per
            stores += copy_all([(replies.at[first:last], replies_hbm.at[first:last])], sems, 1 + c)
            stores[-1].start()
    wait(stores)


def field_kernel(field0, g_high, g_low, returned, field, spread):
    values = returned[...]
    found = (field0[...] - (mm(g_high[...], values) + mm(g_low[...], values))).astype(BF16)
    field[...] = found
    for r in range(spread.shape[0]):
        spread[r] = found


def hess_kernel(me_ref, pair, *refs):
    others, col_tile, hess = refs[:-5], refs[-5], refs[-4]
    row_tile, tiles, sems = refs[-3:]
    scale = 1.0 / col_tile.shape[1]
    me = me_ref[0]
    slots, height, _ = tiles.shape
    for d, block in enumerate((pair,) + others):
        for k in range(2):
            row_tile[me ^ (2 * d + k)] = block[k]
    rows = row_tile[...].reshape(-1, col_tile.shape[1])
    columns = col_tile[...]
    copies = []
    for t in range(hess.shape[0] // height):
        slot = t % slots
        if t >= slots:
            copies[t - slots].wait()
        at = slice(t * height, (t + 1) * height)
        gram = mm(rows[at, :], columns, NT) * scale
        tiles[slot] = gram * gram
        copies += copy_all([(tiles.at[slot], hess.at[at])], sems, slot)
        copies[-1].start()
    wait(copies[-slots:])


def call(kernel, outs, ins, scratch, specs, out_specs, flops, moved, vmem):
    return pl.pallas_call(
        kernel,
        out_shape=outs,
        in_specs=specs,
        out_specs=out_specs,
        scratch_shapes=scratch,
        compiler_params=pltpu.CompilerParams(vmem_limit_bytes=int(vmem * 1024 * 1024)),
        cost_estimate=pl.CostEstimate(flops=flops, bytes_accessed=moved, transcendentals=0),
    )(*ins)


def local(
    rhs, front_factor, coupling, bound_count, sep_owner, sep_index, sep_rhs, sep_factor,
    cell_weight, cell_pivot,
):
    row_count = lax.axis_size("row")
    col_count = lax.axis_size("col")
    fronts = row_count * col_count
    bound, order = coupling.shape
    sources = rhs.shape[1]
    sep_size = sep_rhs.shape[0]
    halves = sep_owner.shape[1]
    cells = cell_weight.shape[0]
    half = order // 2
    flat = fronts * PAD
    vm = pl.BlockSpec(memory_space=VMEM)
    sm = pl.BlockSpec(memory_space=SMEM)
    hbm = pl.BlockSpec(memory_space=pl.ANY)
    shape = jax.ShapeDtypeStruct

    dma = pltpu.SemaphoreType.DMA
    both = ("row", "col")
    me = lax.axis_index("col").astype(jnp.int32).reshape(1)
    outgoing, inv_high, inv_low = call(
        forward_kernel,
        (
            shape((fronts, PAD, sources), BF16),
            shape((2, half, half), BF16),
            shape((2, half, half), BF16),
        ),
        (sep_owner, bound_count, me, sep_index, front_factor, rhs, coupling),
        [
            VMEM((order // BASE, BASE, BASE), F32),
            VMEM((2, BASE, BASE), F32),
            VMEM((half, half), F32),
            VMEM((order, sources), F32),
            VMEM((bound, order), BF16),
            VMEM((2, half, half), BF16),
            VMEM((2, half, half), BF16),
            VMEM((bound + 8, sources), F32),
            VMEM((fronts, PAD, sources), BF16),
            dma((9,)),
        ],
        [sm, sm, sm, vm, hbm, hbm, hbm],
        (hbm,) * 3,
        8_000_000_000,
        14_000_000,
        58,
    )

    def exchange(blocks):
        return lax.all_to_all(
            blocks, both, split_axis=0, concat_axis=0, tiled=True
        )

    incoming = exchange(outgoing)
    schur = call(
        schur_kernel,
        shape((sep_size, sep_size + sources), F32),
        (sep_factor, sep_rhs),
        [VMEM((sep_size, sep_size), F32), dma((2,))],
        [hbm, hbm],
        vm,
        2_000_000_000,
        3_000_000,
        24,
    )
    field0, g_high, g_low = call(
        project_kernel,
        (
            shape((cells, sources), F32),
            shape((cells, flat), BF16),
            shape((cells, flat), BF16),
        ),
        (
            sep_owner, bound_count, front_factor, rhs, coupling, inv_high, inv_low,
            cell_weight, cell_pivot,
        ),
        [
            VMEM((half, half), F32),
            VMEM((order, sources), F32),
            VMEM((bound, order), BF16),
            VMEM((2, half, half), BF16),
            VMEM((2, half, half), BF16),
            VMEM((bound + 8, cells), F32),
            VMEM((fronts, PAD, cells), F32),
            dma((5,)),
        ],
        [sm, sm, hbm, hbm, hbm, hbm, hbm, vm, vm],
        (vm,) * 3,
        4_000_000_000,
        11_000_000,
        36,
    )
    schur, _ = lax.optimization_barrier((schur, g_high))
    sep_potential, replies = call(
        lambda *refs: separator_kernel(*refs, slots=bound // halves),
        (shape((sep_size, sources), F32), shape((fronts, PAD, sources), BF16)),
        (incoming, schur),
        [
            VMEM((sep_size, sep_size + sources), F32),
            VMEM((sep_size, sources), F32),
            VMEM((fronts, PAD, sources), BF16),
            dma((flat // WIDE + 1,)),
        ],
        [vm, hbm],
        (hbm, hbm),
        3_000_000_000,
        5_000_000,
        FULL,
    )
    returned = exchange(replies).reshape(flat, sources)
    field, spread = call(
        field_kernel,
        (shape((cells, sources), BF16), shape((row_count, cells, sources), BF16)),
        (field0, g_high, g_low, returned),
        [],
        [vm] * 4,
        (vm, vm),
        600_000_000,
        5_000_000,
        16,
    )
    col_tile = lax.all_to_all(
        spread, "row", split_axis=0, concat_axis=0, tiled=True
    ).reshape(row_count * cells, sources)
    mate = lax.ppermute(field, "col", [(i, i ^ 1) for i in range(col_count)])
    pair = jnp.stack([field, mate])
    others = [
        lax.ppermute(pair, "col", [(i, i ^ (2 * d)) for i in range(col_count)])
        for d in range(1, col_count // 2)
    ]
    hess = call(
        hess_kernel,
        shape((col_count * cells, row_count * cells), F32),
        (me, pair, *others, col_tile),
        [
            VMEM((col_count, cells, sources), BF16),
            VMEM((4, BASE, row_count * cells), F32),
            dma((4,)),
        ],
        [sm] + [vm] * (col_count // 2 + 1),
        hbm,
        1_000_000_000,
        10_000_000,
        24,
    )
    return (sep_potential, hess)


def solution(mesh):
    placed = P(("row", "col"), None)
    return jax.shard_map(
        local,
        mesh=mesh,
        in_specs=(placed, placed, placed, P(("row", "col"))) + (placed,) * 6,
        out_specs=(placed, P("row", "col")),
        check_vma=False,
    )
```

```python
import jax
import jax.numpy as jnp
from jax import lax
from jax.experimental import pallas as pl
from jax.experimental.pallas import tpu as pltpu
from jax.sharding import PartitionSpec as P

F32 = jnp.float32
BF16 = jnp.bfloat16
NN = (((1,), (0,)), ((), ()))
NT = (((1,), (1,)), ((), ()))
UNIT = 128
BASE = 256
WIDE = 512
PAD = 32
LANES = 128
VMEM = pltpu.VMEM
SMEM = pltpu.SMEM


def mm(a, b, dims=NN):
    return lax.dot_general(a, b, dims, preferred_element_type=F32)


def split(x):
    high = x.astype(BF16)
    return high, (x - high.astype(F32)).astype(BF16)


def mm3(a, b, dims=NN):
    return mm(a[0], b[0], dims) + (mm(a[0], b[1], dims) + mm(a[1], b[0], dims))


def side_by_side(first, second):
    return jnp.concatenate([first, second], axis=1)


def on_diagonal(pair):
    order = pair.shape[0]
    zero = jnp.zeros((order, order), pair.dtype)
    return jnp.concatenate(
        [side_by_side(pair[:, :order], zero), side_by_side(zero, pair[:, order:])], axis=0
    )


def mm_pair(a, b):
    return mm3(a, (on_diagonal(b[0]), on_diagonal(b[1])))


def invert_lower(read, count, midway=None):
    row = lax.broadcasted_iota(jnp.int32, (UNIT, 2 * UNIT), 0)
    col = lax.broadcasted_iota(jnp.int32, (UNIT, 2 * UNIT), 1) & (UNIT - 1)
    first = lax.broadcasted_iota(jnp.int32, (UNIT, 2 * UNIT), 1) < UNIT

    def below(level):
        same = (row >> (level + 1)) == (col >> (level + 1))
        return same & (((row >> level) & 1) == 1) & (((col >> level) & 1) == 0)

    pairs = [side_by_side(read(b, 0, 0), read(b, 1, 1)) for b in range(count)]
    found = []
    mask = below(0)
    for pair in pairs:
        diagonal = jnp.where(row == col, pair, 0.0)
        across = 1.0 / jnp.where(row == col, pair, 1.0)
        across = jnp.sum(jnp.where(row == col, across, 0.0), axis=0, keepdims=True)
        down = 1.0 / jnp.where(
            first,
            jnp.sum(diagonal[:, :UNIT], axis=1, keepdims=True),
            jnp.sum(diagonal[:, UNIT:], axis=1, keepdims=True),
        )
        below_it = jnp.where(mask, -(down * pair * across), 0.0)
        found.append(jnp.where(row == col, down, below_it))
    level = 1
    while (1 << level) < UNIT:
        if level == 3 and midway is not None:
            midway()
        mask = below(level)
        parts = [split(one) for one in found]
        halves = [mm_pair(p, split(jnp.where(mask, pair, 0.0))) for p, pair in zip(parts, pairs)]
        found = [one - mm_pair(split(h), p) for one, h, p in zip(found, halves, parts)]
        level += 1
    result = []
    for b in range(0, count, 2):
        left, right = found[b], found[b + 1]
        tops = split(side_by_side(left[:, :UNIT], right[:, :UNIT]))
        ends = split(side_by_side(left[:, UNIT:], right[:, UNIT:]))
        between = split(side_by_side(read(b, 1, 0), read(b + 1, 1, 0)))
        corners = -mm_pair(ends, split(mm_pair(between, tops)))
        zero = jnp.zeros((UNIT, UNIT), F32)
        for k, one in enumerate((left, right)):
            corner = corners[:, k * UNIT : (k + 1) * UNIT]
            result.append(
                jnp.concatenate(
                    [side_by_side(one[:, :UNIT], zero), side_by_side(corner, one[:, UNIT:])], axis=0
                )
            )
    return result


def solve_rows(rows, high, low, off):
    half = off[0].shape[0]
    inv = [(high[i], low[i]) for i in range(2)]
    x0 = mm3(split(rows[:, :half]), inv[0], NT)
    x1 = mm3(split(rows[:, half:] - mm3(split(x0), off, NT)), inv[1], NT)
    y1 = mm3(split(x1), inv[1])
    y0 = mm3(split(x0 - mm3(split(y1), off)), inv[0])
    return y0, y1


def copy_all(pairs, sems, first=0):
    return [
        pltpu.make_async_copy(source, target, sems.at[first + k])
        for k, (source, target) in enumerate(pairs)
    ]


def start(copies):
    for copy in copies:
        copy.start()


def wait(copies):
    for copy in copies:
        copy.wait()


def place_rows(source, target, owner_ref, count, slots, halves, extra=None, again=0):
    width = target.shape[2]
    spare = PAD - slots
    row = lax.broadcasted_iota(jnp.int32, (PAD, width), 0)
    for j in range(halves):
        live = jnp.minimum(count - slots * j, slots)
        first = slots * j + again
        rows = source[first : first + PAD, :]
        keep = row < live
        if again:
            rows = jnp.where(row < slots, rows, source[first - spare : first - spare + PAD, :])
            keep = jnp.where(row < slots, row, row - spare) < live
        rows = jnp.where(keep, rows, 0.0)
        if extra is not None:
            rows = jnp.where(row == slots, extra[j : j + 1, :], rows)
        target[owner_ref[0, j]] = rows.astype(target.dtype)


def one_hot(cond):
    return jnp.where(cond, 1.0, 0.0).astype(BF16)


def group_of(row):
    return (row * 2341) >> 16


def forward_kernel(
    owner_ref, count_ref, me_ref, index, factor, rhs, coupling,
    out_hbm, high_out, low_out,
    diag, between, lower, right, block, high, low, contrib, out, sems,
):
    quarters = diag.shape[0]
    half = lower.shape[0]
    bound = coupling.shape[0]
    halves = owner_ref.shape[1]
    slots = bound // halves
    pieces = 4

    def tile(i, k):
        return factor.at[i * BASE : (i + 1) * BASE, k * BASE : (k + 1) * BASE]

    factor_copies = copy_all([(tile(k, k), diag.at[k]) for k in range(quarters)], sems)
    rest_copies = copy_all(
        [(tile(2 * i + 1, 2 * i), between.at[i]) for i in range(2)]
        + [(rhs, right), (factor.at[half : 2 * half, 0:half], lower), (coupling, block)],
        sems,
        quarters,
    )
    start(factor_copies + rest_copies)
    out[...] = jnp.zeros_like(out)
    contrib[bound:, :] = jnp.zeros((contrib.shape[0] - bound, contrib.shape[1]), F32)
    mine = group_of(lax.broadcasted_iota(jnp.int32, (halves, bound), 1)) == (
        lax.broadcasted_iota(jnp.int32, (halves, bound), 0)
    )
    values = index[...]
    low_bits = jnp.where(mine, (values & 255).astype(F32), 0.0).astype(BF16)
    high_bits = jnp.where(mine, ((values >> 8) + 1).astype(F32), 0.0).astype(BF16)
    at = lax.broadcasted_iota(jnp.int32, (bound, LANES), 0)
    lane = lax.broadcasted_iota(jnp.int32, (bound, LANES), 1)
    part = me_ref[0] & (LANES // PAD - 1)
    fold = one_hot((at - slots * group_of(at)) + PAD * part == lane)
    extra = side_by_side(mm(low_bits, fold), mm(high_bits, fold))
    wait(factor_copies)

    def read(b, i, k):
        return diag[b, i * UNIT : (i + 1) * UNIT, k * UNIT : (k + 1) * UNIT]

    sides = []

    def midway():
        wait(rest_copies[:4])
        sides.extend((right[...].T, split(lower[...])))

    inverses = invert_lower(read, quarters, midway)
    for i in range(2):
        first_parts, second_parts = split(inverses[2 * i]), split(inverses[2 * i + 1])
        corner = split(-mm3(second_parts, split(mm3(split(between[i]), first_parts))))
        for k, ref in enumerate((high, low)):
            ref[i, :BASE, :BASE] = first_parts[k]
            ref[i, BASE:, BASE:] = second_parts[k]
            ref[i, BASE:, :BASE] = corner[k]
            ref[i, :BASE, BASE:] = jnp.zeros((BASE, BASE), BF16)
    keep = copy_all([(high, high_out), (low, low_out)], sems)
    start(keep)
    y0, y1 = solve_rows(sides[0], high, low, sides[1])
    wait(rest_copies[4:])
    contrib[:bound, :] = mm(block[:, :half], y0.astype(BF16), NT) + mm(
        block[:, half:], y1.astype(BF16), NT
    )
    place_rows(contrib, out, owner_ref, count_ref[0], slots, halves, extra)
    size = out.shape[0] // pieces
    send = copy_all(
        [
            (out.at[k * size : (k + 1) * size], out_hbm.at[k * size : (k + 1) * size])
            for k in range(pieces)
        ],
        sems,
        quarters,
    )
    start(send)
    wait(keep)
    wait(send)


def schur_kernel(sep_hbm, rhs_hbm, both, sep, sems):
    order = sep.shape[0]
    copies = copy_all([(sep_hbm, sep), (rhs_hbm, both.at[:, order:])], sems)
    start(copies)
    copies[0].wait()

    def read(b, i, k):
        top = b * BASE
        return sep[top + i * UNIT : top + (i + 1) * UNIT, top + k * UNIT : top + (k + 1) * UNIT]

    first, second = invert_lower(read, 2)
    first_parts, second_parts = split(first), split(second)
    corner = -mm3(second_parts, split(mm3(split(sep[BASE:, :BASE]), first_parts)))
    corner_parts = split(corner)
    first_t, second_t, corner_t = split(first.T), split(second.T), split(corner.T)
    pieces = (
        (0, 0, mm3(first_t, first_parts) + mm3(corner_t, corner_parts)),
        (0, 1, mm3(corner_t, second_parts)),
        (1, 0, mm3(second_t, corner_parts)),
        (1, 1, mm3(second_t, second_parts)),
    )
    for i, k, piece in pieces:
        at = (slice(i * BASE, (i + 1) * BASE), slice(k * BASE, (k + 1) * BASE))
        both[at] = piece
    copies[1].wait()


def project_kernel(
    owner_ref, count_ref, factor, rhs, coupling, high_hbm, low_hbm, weight, pivot,
    field0, g_high, g_low,
    lower, right, block, high, low, rows, placed, sems,
):
    half = lower.shape[0]
    bound = coupling.shape[0]
    halves = owner_ref.shape[1]
    cells = weight.shape[0]
    copies = [
        pltpu.make_async_copy(high_hbm, high, sems.at[0]),
        pltpu.make_async_copy(low_hbm, low, sems.at[1]),
        pltpu.make_async_copy(factor.at[half : 2 * half, 0:half], lower, sems.at[2]),
        pltpu.make_async_copy(rhs, right, sems.at[3]),
        pltpu.make_async_copy(coupling, block, sems.at[4]),
    ]
    for copy in copies:
        copy.start()
    placed[...] = jnp.zeros_like(placed)
    places = lax.broadcasted_iota(jnp.int32, (cells, 2 * half), 1)
    project = jnp.zeros((cells, 2 * half), F32)
    for k in range(weight.shape[1]):
        project += jnp.where(places == pivot[:, k : k + 1], weight[:, k : k + 1], 0.0)
    for copy in copies[:3]:
        copy.wait()
    y0, y1 = solve_rows(project, high, low, split(lower[...]))
    y0, y1 = split(y0), split(y1)
    copies[3].wait()
    field0[...] = mm3(y0, split(right[:half, :])) + mm3(y1, split(right[half:, :]))
    copies[4].wait()
    both = mm(block[:, :half], jnp.concatenate(y0, axis=0), NT) + mm(
        block[:, half:], jnp.concatenate(y1, axis=0), NT
    )
    rows[:8, :] = jnp.zeros((8, cells), F32)
    rows[8 : 8 + bound, :] = both[:, :cells] + both[:, cells:]
    rows[8 + bound :, :] = jnp.zeros((rows.shape[0] - bound - 8, cells), F32)
    place_rows(rows, placed, owner_ref, count_ref[0], bound // halves, halves, again=8)
    group = LANES // PAD
    for t in range(placed.shape[0] // group):
        tile = placed[t * group : (t + 1) * group].reshape(LANES, cells).T
        g_high[:, t * LANES : (t + 1) * LANES], g_low[:, t * LANES : (t + 1) * LANES] = split(tile)


def pick(cond):
    return jnp.where(cond, jnp.ones((), BF16), jnp.zeros((), BF16))


def fold_halves(blocks, slots):
    left, right = blocks[:, :, :LANES], blocks[:, :, LANES:]
    whole = slots // 8 * 8
    pieces = []
    for top in range(0, whole, 8):
        pieces += [left[:, top : top + 8], right[:, top : top + 8]]
    row = lax.broadcasted_iota(jnp.int32, (blocks.shape[0], 8, LANES), 1)
    pieces.append(jnp.where(row < slots - whole, left[:, whole:], right[:, whole:]))
    return jnp.concatenate(pieces, axis=1)


def unfold_halves(folded, slots):
    whole = slots // 8 * 8
    shared = folded[:, 2 * whole :]
    row = lax.broadcasted_iota(jnp.int32, shared.shape, 1)
    left = [folded[:, 2 * top : 2 * top + 8] for top in range(0, whole, 8)]
    right = [folded[:, 2 * top + 8 : 2 * top + 16] for top in range(0, whole, 8)]
    left.append(jnp.where(row < slots - whole, shared, 0.0))
    right.append(jnp.where(row < slots - whole, 0.0, shared))
    return jnp.concatenate(
        [jnp.concatenate(left, axis=1), jnp.concatenate(right, axis=1)], axis=2
    )


def separator_kernel(
    incoming, schur_hbm, potential, replies, schur, sems, *, slots
):
    fronts = incoming.shape[0]
    chunks = fronts * PAD // WIDE
    per = WIDE // PAD
    rest = copy_all([(schur_hbm, schur)], sems)
    start(rest)
    group = LANES // PAD
    tail = incoming[:, PAD - 8 :, :].astype(F32)
    tail = tail.reshape(fronts // group, group, 8, -1)
    tail = (tail[:, 0] + tail[:, 1]) + (tail[:, 2] + tail[:, 3])
    tail = tail[:, slots - (PAD - 8), :]
    low_bits, high_bits = tail[:, :LANES], tail[:, LANES:]
    rows = [jnp.where(high_bits == 1.0 + p, low_bits, -1.0) for p in range(2)]
    empty = jnp.full((LANES - rows[0].shape[0], LANES), -1.0, F32)
    spare = PAD - slots
    last = (lax.broadcasted_iota(jnp.int32, rows[0].shape, 1) & (PAD - 1)) >= slots
    twice = [jnp.where(last, pltpu.roll(one, spare, 1), one) for one in rows]
    cols = [jnp.concatenate([one, empty], axis=0).T for one in twice]
    order = schur.shape[0]
    part = order // 2
    down = lax.broadcasted_iota(jnp.int32, (part, LANES), 0).astype(F32).astype(BF16)
    along = lax.broadcasted_iota(jnp.int32, (LANES, part), 1).astype(F32).astype(BF16)
    each = WIDE // LANES
    total = None
    for c in range(chunks):
        tiles = [
            jnp.concatenate(
                [pick(down == rows[p][g : g + 1, :].astype(BF16)) for p in range(2)], axis=0
            )
            for g in range(c * each, (c + 1) * each)
        ]
        values = incoming[c * per : (c + 1) * per].reshape(WIDE, -1)
        term = mm(jnp.concatenate(tiles, axis=1), values)
        total = term if total is None else total + term
    wait(rest)
    found = mm3(split(schur[:, :order]), split(schur[:, order:] - total))
    potential[...] = found
    rounded = found.astype(BF16)
    for c in range(chunks):
        tiles = [
            jnp.concatenate(
                [pick(along == cols[p][:, g : g + 1].astype(BF16)) for p in range(2)], axis=1
            )
            for g in range(c * each, (c + 1) * each)
        ]
        chosen = jnp.concatenate(tiles, axis=0)
        blocks = mm(chosen, rounded).reshape(per, PAD, rounded.shape[1])
        replies[c * per : (c + 1) * per] = fold_halves(blocks, slots).astype(BF16)


def field_kernel(field0, g_high, g_low, returned, field, spread, *, slots):
    values = unfold_halves(returned[...].astype(F32), slots).astype(BF16)
    values = values.reshape(g_high.shape[1], -1)
    found = (field0[...] - (mm(g_high[...], values) + mm(g_low[...], values))).astype(BF16)
    field[...] = found
    for r in range(spread.shape[0]):
        spread[r] = found


def hess_kernel(me_ref, pair, *refs):
    others, col_tile, hess = refs[:-5], refs[-5], refs[-4]
    row_tile, tiles, sems = refs[-3:]
    scale = 1.0 / col_tile.shape[1]
    me = me_ref[0]
    slots, height, _ = tiles.shape
    for d, block in enumerate((pair,) + others):
        for k in range(2):
            row_tile[me ^ (2 * d + k)] = block[k]
    rows = row_tile[...].reshape(-1, col_tile.shape[1])
    columns = col_tile[...]
    copies = []
    for t in range(hess.shape[0] // height):
        slot = t % slots
        if t >= slots:
            copies[t - slots].wait()
        at = slice(t * height, (t + 1) * height)
        gram = mm(rows[at, :], columns, NT) * scale
        tiles[slot] = gram * gram
        copies += copy_all([(tiles.at[slot], hess.at[at])], sems, slot)
        copies[-1].start()
    wait(copies[-slots:])


def call(kernel, outs, ins, scratch, specs, out_specs, flops, moved, vmem):
    return pl.pallas_call(
        kernel,
        out_shape=outs,
        in_specs=specs,
        out_specs=out_specs,
        scratch_shapes=scratch,
        compiler_params=pltpu.CompilerParams(vmem_limit_bytes=int(vmem * 1024 * 1024)),
        cost_estimate=pl.CostEstimate(flops=flops, bytes_accessed=moved, transcendentals=0),
    )(*ins)


def local(
    rhs, front_factor, coupling, bound_count, sep_owner, sep_index, sep_rhs, sep_factor,
    cell_weight, cell_pivot,
):
    row_count = lax.axis_size("row")
    col_count = lax.axis_size("col")
    fronts = row_count * col_count
    bound, order = coupling.shape
    sources = rhs.shape[1]
    sep_size = sep_rhs.shape[0]
    halves = sep_owner.shape[1]
    cells = cell_weight.shape[0]
    half = order // 2
    slots = bound // halves
    flat = fronts * PAD
    vm = pl.BlockSpec(memory_space=VMEM)
    sm = pl.BlockSpec(memory_space=SMEM)
    hbm = pl.BlockSpec(memory_space=pl.ANY)
    shape = jax.ShapeDtypeStruct

    dma = pltpu.SemaphoreType.DMA
    both = ("row", "col")
    me = lax.axis_index("col").astype(jnp.int32).reshape(1)
    outgoing, inv_high, inv_low = call(
        forward_kernel,
        (
            shape((fronts, PAD, sources), BF16),
            shape((2, half, half), BF16),
            shape((2, half, half), BF16),
        ),
        (sep_owner, bound_count, me, sep_index, front_factor, rhs, coupling),
        [
            VMEM((order // BASE, BASE, BASE), F32),
            VMEM((2, BASE, BASE), F32),
            VMEM((half, half), F32),
            VMEM((order, sources), F32),
            VMEM((bound, order), BF16),
            VMEM((2, half, half), BF16),
            VMEM((2, half, half), BF16),
            VMEM((bound + 8, sources), F32),
            VMEM((fronts, PAD, sources), BF16),
            dma((9,)),
        ],
        [sm, sm, sm, vm, hbm, hbm, hbm],
        (hbm,) * 3,
        8_000_000_000,
        14_000_000,
        58,
    )

    def exchange(blocks):
        return lax.all_to_all(
            blocks, both, split_axis=0, concat_axis=0, tiled=True
        )

    incoming = exchange(outgoing)
    schur = call(
        schur_kernel,
        shape((sep_size, sep_size + sources), F32),
        (sep_factor, sep_rhs),
        [VMEM((sep_size, sep_size), F32), dma((2,))],
        [hbm, hbm],
        vm,
        2_000_000_000,
        3_000_000,
        24,
    )
    field0, g_high, g_low = call(
        project_kernel,
        (
            shape((cells, sources), F32),
            shape((cells, flat), BF16),
            shape((cells, flat), BF16),
        ),
        (
            sep_owner, bound_count, front_factor, rhs, coupling, inv_high, inv_low,
            cell_weight, cell_pivot,
        ),
        [
            VMEM((half, half), F32),
            VMEM((order, sources), F32),
            VMEM((bound, order), BF16),
            VMEM((2, half, half), BF16),
            VMEM((2, half, half), BF16),
            VMEM((bound + 16, cells), F32),
            VMEM((fronts, PAD, cells), F32),
            dma((5,)),
        ],
        [sm, sm, hbm, hbm, hbm, hbm, hbm, vm, vm],
        (vm,) * 3,
        4_000_000_000,
        11_000_000,
        36,
    )
    schur, _ = lax.optimization_barrier((schur, g_high))
    sep_potential, replies = call(
        lambda *refs: separator_kernel(*refs, slots=slots),
        (shape((sep_size, sources), F32), shape((fronts, 2 * slots, LANES), BF16)),
        (incoming, schur),
        [
            VMEM((sep_size, sep_size + sources), F32),
            dma((1,)),
        ],
        [vm, hbm],
        (vm, vm),
        3_000_000_000,
        5_000_000,
        28,
    )
    returned = exchange(replies)
    field, spread = call(
        lambda *refs: field_kernel(*refs, slots=slots),
        (shape((cells, sources), BF16), shape((row_count, cells, sources), BF16)),
        (field0, g_high, g_low, returned),
        [],
        [vm] * 4,
        (vm, vm),
        600_000_000,
        5_000_000,
        16,
    )
    col_tile = lax.all_to_all(
        spread, "row", split_axis=0, concat_axis=0, tiled=True
    ).reshape(row_count * cells, sources)
    mate = lax.ppermute(field, "col", [(i, i ^ 1) for i in range(col_count)])
    pair = jnp.stack([field, mate])
    others = [
        lax.ppermute(pair, "col", [(i, i ^ (2 * d)) for i in range(col_count)])
        for d in range(1, col_count // 2)
    ]
    hess = call(
        hess_kernel,
        shape((col_count * cells, row_count * cells), F32),
        (me, pair, *others, col_tile),
        [
            VMEM((col_count, cells, sources), BF16),
            VMEM((4, BASE, row_count * cells), F32),
            dma((4,)),
        ],
        [sm] + [vm] * (col_count // 2 + 1),
        hbm,
        1_000_000_000,
        10_000_000,
        24,
    )
    return (sep_potential, hess)


def solution(mesh):
    placed = P(("row", "col"), None)
    return jax.shard_map(
        local,
        mesh=mesh,
        in_specs=(placed, placed, placed, P(("row", "col"))) + (placed,) * 6,
        out_specs=(placed, P("row", "col")),
        check_vma=False,
    )
```

```python
import jax
import jax.numpy as jnp
from jax import lax
from jax.experimental import pallas as pl
from jax.experimental.pallas import tpu as pltpu
from jax.sharding import PartitionSpec as P

F32 = jnp.float32
BF16 = jnp.bfloat16
NN = (((1,), (0,)), ((), ()))
NT = (((1,), (1,)), ((), ()))
UNIT = 128
BASE = 256
WIDE = 512
PAD = 32
LANES = 128
VMEM = pltpu.VMEM
SMEM = pltpu.SMEM


def mm(a, b, dims=NN):
    return lax.dot_general(a, b, dims, preferred_element_type=F32)


def split(x):
    high = x.astype(BF16)
    return high, (x - high.astype(F32)).astype(BF16)


def mm3(a, b, dims=NN):
    return mm(a[0], b[0], dims) + (mm(a[0], b[1], dims) + mm(a[1], b[0], dims))


def side_by_side(first, second):
    return jnp.concatenate([first, second], axis=1)


def on_diagonal(pair):
    order = pair.shape[0]
    zero = jnp.zeros((order, order), pair.dtype)
    return jnp.concatenate(
        [side_by_side(pair[:, :order], zero), side_by_side(zero, pair[:, order:])], axis=0
    )


def mm_pair(a, b):
    return mm3(a, (on_diagonal(b[0]), on_diagonal(b[1])))


def invert_lower(read, count, midway=None):
    row = lax.broadcasted_iota(jnp.int32, (UNIT, 2 * UNIT), 0)
    col = lax.broadcasted_iota(jnp.int32, (UNIT, 2 * UNIT), 1) & (UNIT - 1)
    first = lax.broadcasted_iota(jnp.int32, (UNIT, 2 * UNIT), 1) < UNIT

    def below(level):
        same = (row >> (level + 1)) == (col >> (level + 1))
        return same & (((row >> level) & 1) == 1) & (((col >> level) & 1) == 0)

    pairs = [side_by_side(read(b, 0, 0), read(b, 1, 1)) for b in range(count)]
    found = []
    mask = below(0)
    for pair in pairs:
        diagonal = jnp.where(row == col, pair, 0.0)
        across = 1.0 / jnp.where(row == col, pair, 1.0)
        across = jnp.sum(jnp.where(row == col, across, 0.0), axis=0, keepdims=True)
        down = 1.0 / jnp.where(
            first,
            jnp.sum(diagonal[:, :UNIT], axis=1, keepdims=True),
            jnp.sum(diagonal[:, UNIT:], axis=1, keepdims=True),
        )
        below_it = jnp.where(mask, -(down * pair * across), 0.0)
        found.append(jnp.where(row == col, down, below_it))
    level = 1
    while (1 << level) < UNIT:
        if level == 3 and midway is not None:
            midway()
        mask = below(level)
        parts = [split(one) for one in found]
        halves = [mm_pair(p, split(jnp.where(mask, pair, 0.0))) for p, pair in zip(parts, pairs)]
        found = [one - mm_pair(split(h), p) for one, h, p in zip(found, halves, parts)]
        level += 1
    result = []
    for b in range(0, count, 2):
        left, right = found[b], found[b + 1]
        tops = split(side_by_side(left[:, :UNIT], right[:, :UNIT]))
        ends = split(side_by_side(left[:, UNIT:], right[:, UNIT:]))
        between = split(side_by_side(read(b, 1, 0), read(b + 1, 1, 0)))
        corners = -mm_pair(ends, split(mm_pair(between, tops)))
        zero = jnp.zeros((UNIT, UNIT), F32)
        for k, one in enumerate((left, right)):
            corner = corners[:, k * UNIT : (k + 1) * UNIT]
            result.append(
                jnp.concatenate(
                    [side_by_side(one[:, :UNIT], zero), side_by_side(corner, one[:, UNIT:])], axis=0
                )
            )
    return result


def solve_rows(rows, high, low, off):
    half = off[0].shape[0]
    inv = [(high[i], low[i]) for i in range(2)]
    x0 = mm3(split(rows[:, :half]), inv[0], NT)
    x1 = mm3(split(rows[:, half:] - mm3(split(x0), off, NT)), inv[1], NT)
    y1 = mm3(split(x1), inv[1])
    y0 = mm3(split(x0 - mm3(split(y1), off)), inv[0])
    return y0, y1


def copy_all(pairs, sems, first=0):
    return [
        pltpu.make_async_copy(source, target, sems.at[first + k])
        for k, (source, target) in enumerate(pairs)
    ]


def start(copies):
    for copy in copies:
        copy.start()


def wait(copies):
    for copy in copies:
        copy.wait()


def place_rows(source, target, owner_ref, count, slots, halves, extra=None, again=0):
    width = target.shape[2]
    spare = PAD - slots
    row = lax.broadcasted_iota(jnp.int32, (PAD, width), 0)
    for j in range(halves):
        live = jnp.minimum(count - slots * j, slots)
        first = slots * j + again
        rows = source[first : first + PAD, :]
        keep = row < live
        if again:
            rows = jnp.where(row < slots, rows, source[first - spare : first - spare + PAD, :])
            keep = jnp.where(row < slots, row, row - spare) < live
        rows = jnp.where(keep, rows, 0.0)
        if extra is not None:
            rows = jnp.where(row == slots, extra[j : j + 1, :], rows)
        target[owner_ref[0, j]] = rows.astype(target.dtype)


def one_hot(cond):
    return jnp.where(cond, 1.0, 0.0).astype(BF16)


def group_of(row):
    return (row * 2341) >> 16


def forward_kernel(
    owner_ref, count_ref, me_ref, index, factor, rhs, coupling,
    out_hbm, high_out, low_out,
    diag, between, lower, right, block, high, low, contrib, out, sems,
):
    quarters = diag.shape[0]
    half = lower.shape[0]
    bound = coupling.shape[0]
    halves = owner_ref.shape[1]
    slots = bound // halves
    pieces = 4

    def tile(i, k):
        return factor.at[i * BASE : (i + 1) * BASE, k * BASE : (k + 1) * BASE]

    factor_copies = copy_all([(tile(k, k), diag.at[k]) for k in range(quarters)], sems)
    rest_copies = copy_all(
        [(tile(2 * i + 1, 2 * i), between.at[i]) for i in range(2)]
        + [(rhs, right), (factor.at[half : 2 * half, 0:half], lower), (coupling, block)],
        sems,
        quarters,
    )
    start(factor_copies + rest_copies)
    out[...] = jnp.zeros_like(out)
    contrib[bound:, :] = jnp.zeros((contrib.shape[0] - bound, contrib.shape[1]), F32)
    mine = group_of(lax.broadcasted_iota(jnp.int32, (halves, bound), 1)) == (
        lax.broadcasted_iota(jnp.int32, (halves, bound), 0)
    )
    values = index[...]
    low_bits = jnp.where(mine, (values & 255).astype(F32), 0.0).astype(BF16)
    high_bits = jnp.where(mine, ((values >> 8) + 1).astype(F32), 0.0).astype(BF16)
    at = lax.broadcasted_iota(jnp.int32, (bound, LANES), 0)
    lane = lax.broadcasted_iota(jnp.int32, (bound, LANES), 1)
    part = me_ref[0] & (LANES // PAD - 1)
    fold = one_hot((at - slots * group_of(at)) + PAD * part == lane)
    extra = side_by_side(mm(low_bits, fold), mm(high_bits, fold))
    wait(factor_copies)

    def read(b, i, k):
        return diag[b, i * UNIT : (i + 1) * UNIT, k * UNIT : (k + 1) * UNIT]

    sides = []

    def midway():
        wait(rest_copies[:4])
        sides.extend((right[...].T, split(lower[...])))

    inverses = invert_lower(read, quarters, midway)
    for i in range(2):
        first_parts, second_parts = split(inverses[2 * i]), split(inverses[2 * i + 1])
        corner = split(-mm3(second_parts, split(mm3(split(between[i]), first_parts))))
        for k, ref in enumerate((high, low)):
            ref[i, :BASE, :BASE] = first_parts[k]
            ref[i, BASE:, BASE:] = second_parts[k]
            ref[i, BASE:, :BASE] = corner[k]
            ref[i, :BASE, BASE:] = jnp.zeros((BASE, BASE), BF16)
    keep = copy_all([(high, high_out), (low, low_out)], sems)
    start(keep)
    y0, y1 = solve_rows(sides[0], high, low, sides[1])
    wait(rest_copies[4:])
    contrib[:bound, :] = mm(block[:, :half], y0.astype(BF16), NT) + mm(
        block[:, half:], y1.astype(BF16), NT
    )
    place_rows(contrib, out, owner_ref, count_ref[0], slots, halves, extra)
    size = out.shape[0] // pieces
    send = copy_all(
        [
            (out.at[k * size : (k + 1) * size], out_hbm.at[k * size : (k + 1) * size])
            for k in range(pieces)
        ],
        sems,
        quarters,
    )
    start(send)
    wait(keep)
    wait(send)


def schur_kernel(sep_hbm, rhs_hbm, both, sep, sems):
    order = sep.shape[0]
    copies = copy_all([(sep_hbm, sep), (rhs_hbm, both.at[:, order:])], sems)
    start(copies)
    copies[0].wait()

    def read(b, i, k):
        top = b * BASE
        return sep[top + i * UNIT : top + (i + 1) * UNIT, top + k * UNIT : top + (k + 1) * UNIT]

    first, second = invert_lower(read, 2)
    first_parts, second_parts = split(first), split(second)
    corner = -mm3(second_parts, split(mm3(split(sep[BASE:, :BASE]), first_parts)))
    corner_parts = split(corner)
    first_t, second_t, corner_t = split(first.T), split(second.T), split(corner.T)
    pieces = (
        (0, 0, mm3(first_t, first_parts) + mm3(corner_t, corner_parts)),
        (0, 1, mm3(corner_t, second_parts)),
        (1, 0, mm3(second_t, corner_parts)),
        (1, 1, mm3(second_t, second_parts)),
    )
    for i, k, piece in pieces:
        at = (slice(i * BASE, (i + 1) * BASE), slice(k * BASE, (k + 1) * BASE))
        both[at] = piece
    copies[1].wait()


def project_kernel(
    owner_ref, count_ref, factor, rhs, coupling, high_hbm, low_hbm, weight, pivot,
    field0, weights,
    lower, right, block, high, low, rows, placed, sems,
):
    half = lower.shape[0]
    bound = coupling.shape[0]
    halves = owner_ref.shape[1]
    cells = weight.shape[0]
    copies = [
        pltpu.make_async_copy(high_hbm, high, sems.at[0]),
        pltpu.make_async_copy(low_hbm, low, sems.at[1]),
        pltpu.make_async_copy(factor.at[half : 2 * half, 0:half], lower, sems.at[2]),
        pltpu.make_async_copy(rhs, right, sems.at[3]),
        pltpu.make_async_copy(coupling, block, sems.at[4]),
    ]
    for copy in copies:
        copy.start()
    placed[...] = jnp.zeros_like(placed)
    places = lax.broadcasted_iota(jnp.int32, (cells, 2 * half), 1)
    project = jnp.zeros((cells, 2 * half), F32)
    for k in range(weight.shape[1]):
        project += jnp.where(places == pivot[:, k : k + 1], weight[:, k : k + 1], 0.0)
    for copy in copies[:3]:
        copy.wait()
    y0, y1 = solve_rows(project, high, low, split(lower[...]))
    y0, y1 = split(y0), split(y1)
    copies[3].wait()
    field0[...] = mm3(y0, split(right[:half, :])) + mm3(y1, split(right[half:, :]))
    copies[4].wait()
    both = mm(block[:, :half], jnp.concatenate(y0, axis=0), NT) + mm(
        block[:, half:], jnp.concatenate(y1, axis=0), NT
    )
    rows[:8, :] = jnp.zeros((8, cells), F32)
    rows[8 : 8 + bound, :] = both[:, :cells] + both[:, cells:]
    rows[8 + bound :, :] = jnp.zeros((rows.shape[0] - bound - 8, cells), F32)
    place_rows(rows, placed, owner_ref, count_ref[0], bound // halves, halves, again=8)
    group = LANES // PAD
    for t in range(placed.shape[0] // group):
        tile = placed[t * group : (t + 1) * group].reshape(LANES, cells).T
        weights[:, t * LANES : (t + 1) * LANES] = jnp.concatenate(split(tile), axis=0)


def pick(cond):
    return jnp.where(cond, jnp.ones((), BF16), jnp.zeros((), BF16))


def fold_halves(blocks, slots):
    left, right = blocks[:, :, :LANES], blocks[:, :, LANES:]
    whole = slots // 8 * 8
    pieces = []
    for top in range(0, whole, 8):
        pieces += [left[:, top : top + 8], right[:, top : top + 8]]
    row = lax.broadcasted_iota(jnp.int32, (blocks.shape[0], 8, LANES), 1)
    pieces.append(jnp.where(row < slots - whole, left[:, whole:], right[:, whole:]))
    return jnp.concatenate(pieces, axis=1)


def unfold_halves(folded, slots):
    whole = slots // 8 * 8
    shared = folded[:, 2 * whole :]
    row = lax.broadcasted_iota(jnp.int32, shared.shape, 1)
    left = [folded[:, 2 * top : 2 * top + 8] for top in range(0, whole, 8)]
    right = [folded[:, 2 * top + 8 : 2 * top + 16] for top in range(0, whole, 8)]
    left.append(jnp.where(row < slots - whole, shared, 0.0))
    right.append(jnp.where(row < slots - whole, 0.0, shared))
    return jnp.concatenate(
        [jnp.concatenate(left, axis=1), jnp.concatenate(right, axis=1)], axis=2
    )


def separator_kernel(
    incoming, schur_hbm, potential, replies, schur, sems, *, slots
):
    fronts = incoming.shape[0]
    chunks = fronts * PAD // WIDE
    per = WIDE // PAD
    rest = copy_all([(schur_hbm, schur)], sems)
    start(rest)
    group = LANES // PAD
    tail = incoming[:, PAD - 8 :, :].astype(F32)
    tail = tail.reshape(fronts // group, group, 8, -1)
    tail = (tail[:, 0] + tail[:, 1]) + (tail[:, 2] + tail[:, 3])
    tail = tail[:, slots - (PAD - 8), :]
    low_bits, high_bits = tail[:, :LANES], tail[:, LANES:]
    rows = [jnp.where(high_bits == 1.0 + p, low_bits, -1.0) for p in range(2)]
    empty = jnp.full((LANES - rows[0].shape[0], LANES), -1.0, F32)
    spare = PAD - slots
    last = (lax.broadcasted_iota(jnp.int32, rows[0].shape, 1) & (PAD - 1)) >= slots
    twice = [jnp.where(last, pltpu.roll(one, spare, 1), one) for one in rows]
    cols = [jnp.concatenate([one, empty], axis=0).T for one in twice]
    order = schur.shape[0]
    part = order // 2
    down = lax.broadcasted_iota(jnp.int32, (part, LANES), 0).astype(F32).astype(BF16)
    along = lax.broadcasted_iota(jnp.int32, (LANES, part), 1).astype(F32).astype(BF16)
    each = WIDE // LANES
    total = None
    for c in range(chunks):
        tiles = [
            jnp.concatenate(
                [pick(down == rows[p][g : g + 1, :].astype(BF16)) for p in range(2)], axis=0
            )
            for g in range(c * each, (c + 1) * each)
        ]
        values = incoming[c * per : (c + 1) * per].reshape(WIDE, -1)
        term = mm(jnp.concatenate(tiles, axis=1), values)
        total = term if total is None else total + term
    wait(rest)
    found = mm3(split(schur[:, :order]), split(schur[:, order:] - total))
    potential[...] = found
    rounded = found.astype(BF16)
    for c in range(chunks):
        tiles = [
            jnp.concatenate(
                [pick(along == cols[p][:, g : g + 1].astype(BF16)) for p in range(2)], axis=1
            )
            for g in range(c * each, (c + 1) * each)
        ]
        chosen = jnp.concatenate(tiles, axis=0)
        blocks = mm(chosen, rounded).reshape(per, PAD, rounded.shape[1])
        replies[c * per : (c + 1) * per] = fold_halves(blocks, slots).astype(BF16)


def field_kernel(field0, weights, returned, field, spread, *, slots):
    values = unfold_halves(returned[...].astype(F32), slots).astype(BF16)
    values = values.reshape(weights.shape[1], -1)
    cells = field0.shape[0]
    both = mm(weights[...], values)
    found = (field0[...] - (both[:cells] + both[cells:])).astype(BF16)
    field[...] = found
    for r in range(spread.shape[0]):
        spread[r] = found


def hess_kernel(me_ref, pair, *refs):
    others, col_tile, hess = refs[:-5], refs[-5], refs[-4]
    row_tile, tiles, sems = refs[-3:]
    scale = 1.0 / col_tile.shape[1]
    me = me_ref[0]
    slots, height, _ = tiles.shape
    for d, block in enumerate((pair,) + others):
        for k in range(2):
            row_tile[me ^ (2 * d + k)] = block[k]
    rows = row_tile[...].reshape(-1, col_tile.shape[1])
    columns = col_tile[...]
    copies = []
    for t in range(hess.shape[0] // height):
        slot = t % slots
        if t >= slots:
            copies[t - slots].wait()
        at = slice(t * height, (t + 1) * height)
        gram = mm(rows[at, :], columns, NT) * scale
        tiles[slot] = gram * gram
        copies += copy_all([(tiles.at[slot], hess.at[at])], sems, slot)
        copies[-1].start()
    wait(copies[-slots:])


def call(kernel, outs, ins, scratch, specs, out_specs, flops, moved, vmem):
    return pl.pallas_call(
        kernel,
        out_shape=outs,
        in_specs=specs,
        out_specs=out_specs,
        scratch_shapes=scratch,
        compiler_params=pltpu.CompilerParams(vmem_limit_bytes=int(vmem * 1024 * 1024)),
        cost_estimate=pl.CostEstimate(flops=flops, bytes_accessed=moved, transcendentals=0),
    )(*ins)


def local(
    rhs, front_factor, coupling, bound_count, sep_owner, sep_index, sep_rhs, sep_factor,
    cell_weight, cell_pivot,
):
    row_count = lax.axis_size("row")
    col_count = lax.axis_size("col")
    fronts = row_count * col_count
    bound, order = coupling.shape
    sources = rhs.shape[1]
    sep_size = sep_rhs.shape[0]
    halves = sep_owner.shape[1]
    cells = cell_weight.shape[0]
    half = order // 2
    slots = bound // halves
    flat = fronts * PAD
    vm = pl.BlockSpec(memory_space=VMEM)
    sm = pl.BlockSpec(memory_space=SMEM)
    hbm = pl.BlockSpec(memory_space=pl.ANY)
    shape = jax.ShapeDtypeStruct

    dma = pltpu.SemaphoreType.DMA
    both = ("row", "col")
    me = lax.axis_index("col").astype(jnp.int32).reshape(1)
    outgoing, inv_high, inv_low = call(
        forward_kernel,
        (
            shape((fronts, PAD, sources), BF16),
            shape((2, half, half), BF16),
            shape((2, half, half), BF16),
        ),
        (sep_owner, bound_count, me, sep_index, front_factor, rhs, coupling),
        [
            VMEM((order // BASE, BASE, BASE), F32),
            VMEM((2, BASE, BASE), F32),
            VMEM((half, half), F32),
            VMEM((order, sources), F32),
            VMEM((bound, order), BF16),
            VMEM((2, half, half), BF16),
            VMEM((2, half, half), BF16),
            VMEM((bound + 8, sources), F32),
            VMEM((fronts, PAD, sources), BF16),
            dma((9,)),
        ],
        [sm, sm, sm, vm, hbm, hbm, hbm],
        (hbm,) * 3,
        8_000_000_000,
        14_000_000,
        58,
    )

    def exchange(blocks):
        return lax.all_to_all(
            blocks, both, split_axis=0, concat_axis=0, tiled=True
        )

    incoming = exchange(outgoing)
    schur = call(
        schur_kernel,
        shape((sep_size, sep_size + sources), F32),
        (sep_factor, sep_rhs),
        [VMEM((sep_size, sep_size), F32), dma((2,))],
        [hbm, hbm],
        vm,
        2_000_000_000,
        3_000_000,
        24,
    )
    field0, weights = call(
        project_kernel,
        (
            shape((cells, sources), F32),
            shape((2 * cells, flat), BF16),
        ),
        (
            sep_owner, bound_count, front_factor, rhs, coupling, inv_high, inv_low,
            cell_weight, cell_pivot,
        ),
        [
            VMEM((half, half), F32),
            VMEM((order, sources), F32),
            VMEM((bound, order), BF16),
            VMEM((2, half, half), BF16),
            VMEM((2, half, half), BF16),
            VMEM((bound + 16, cells), F32),
            VMEM((fronts, PAD, cells), F32),
            dma((5,)),
        ],
        [sm, sm, hbm, hbm, hbm, hbm, hbm, vm, vm],
        (vm,) * 2,
        4_000_000_000,
        11_000_000,
        36,
    )
    schur, _ = lax.optimization_barrier((schur, weights))
    sep_potential, replies = call(
        lambda *refs: separator_kernel(*refs, slots=slots),
        (shape((sep_size, sources), F32), shape((fronts, 2 * slots, LANES), BF16)),
        (incoming, schur),
        [
            VMEM((sep_size, sep_size + sources), F32),
            dma((1,)),
        ],
        [vm, hbm],
        (vm, vm),
        3_000_000_000,
        5_000_000,
        28,
    )
    returned = exchange(replies)
    field, spread = call(
        lambda *refs: field_kernel(*refs, slots=slots),
        (shape((cells, sources), BF16), shape((row_count, cells, sources), BF16)),
        (field0, weights, returned),
        [],
        [vm] * 3,
        (vm, vm),
        600_000_000,
        5_000_000,
        16,
    )
    col_tile = lax.all_to_all(
        spread, "row", split_axis=0, concat_axis=0, tiled=True
    ).reshape(row_count * cells, sources)
    mate = lax.ppermute(field, "col", [(i, i ^ 1) for i in range(col_count)])
    pair = jnp.stack([field, mate])
    others = [
        lax.ppermute(pair, "col", [(i, i ^ (2 * d)) for i in range(col_count)])
        for d in range(1, col_count // 2)
    ]
    hess = call(
        hess_kernel,
        shape((col_count * cells, row_count * cells), F32),
        (me, pair, *others, col_tile),
        [
            VMEM((col_count, cells, sources), BF16),
            VMEM((4, BASE, row_count * cells), F32),
            dma((4,)),
        ],
        [sm] + [vm] * (col_count // 2 + 1),
        hbm,
        1_000_000_000,
        10_000_000,
        24,
    )
    return (sep_potential, hess)


def solution(mesh):
    placed = P(("row", "col"), None)
    return jax.shard_map(
        local,
        mesh=mesh,
        in_specs=(placed, placed, placed, P(("row", "col"))) + (placed,) * 6,
        out_specs=(placed, P("row", "col")),
        check_vma=False,
    )
```
